256 devices in a mesh: down: 64 (over x, z_hi, y), cross: 4 (over z_lo, core).
Axes of the slice: x: 4, y: 4, z: 8 (z_hi: 4, z_lo: 2; z = z_hi * 2 + z_lo), core: 2. Of those that a mesh axis runs over, the one named last changes fastest.
Arguments:
- fields: float32 [4, 512, 256, 128], P(None, 'down', 'cross'), may hold values from -4 to 4
- embers: float32 [7, 64, 4, 6, 256], P(None, 'down', 'cross'), may hold values from 0.05 to 1
- counts: int32 [64, 4, 6], P('down', 'cross'), may hold values from 0 to 256, as said below
Outputs:
- advanced: float32 [4, 512, 256, 128], P(None, 'down', 'cross')
- landed: float32 [4, 64, 4, 6, 256], P(None, 'down', 'cross')
The draws below stay inside these ranges and needn't reach their ends.
Inputs may be any that keep to these rules, and one draw needn't show every extreme that they name: `counts`: live records fill the leading slots of a buffer; some buffer is full in every draw.
All inputs are finite; a program needn't handle non-finite values.
Results may differ from the reference program's by a relative error of at most 0.0003.
Values sent between devices are 32-bit elements; how exact they have to be, the bound alone decides.
No kernel may reach another device: no remote copies, remote signals or barrier semaphores. Data moves between devices by JAX's collectives and lax.ppermute only.
A program may use at most 64 MiB of HBM per device.

```python
import jax
import jax.numpy as jnp
from jax import lax

CX = 8
CY = 64
NZ = 128
STEPS = 6
SLOTS = 6
CAP = 256
TD = 64
TC = 4
NX = 512
NY = 256


def draw_counts(key, part):
    band_key, front_key, quiet_key = jax.random.split(key, 3)
    band_start = jax.random.randint(band_key, (), 0, TD)
    band_width = max(1, TD // 8)
    tile_rows = jnp.arange(TD)[:, None, None]
    in_front = (tile_rows - band_start) % TD < band_width
    front_counts = jax.random.randint(front_key, (TD, TC, SLOTS), CAP // 2, CAP + 1)
    quiet_counts = jax.random.randint(quiet_key, (TD, TC, SLOTS), 0, CAP // 4 + 1)
    counts = jnp.where(in_front, front_counts, quiet_counts)
    full_slot = (tile_rows == band_start) & (jnp.arange(TC)[None, :, None] == 0) & (jnp.arange(SLOTS)[None, None, :] == 0)
    return jnp.where(full_slot, CAP, counts).astype(jnp.int32)


def level_of(stream_key, dims, cuts, low, largest):
    loudness, own = 1.0, jax.random.fold_in(stream_key, 6)
    for dim, shards_of in cuts:
        draws = jnp.exp(jax.random.uniform(jax.random.fold_in(own, dim), (shards_of,), jnp.float32, low / len(cuts), largest / len(cuts)))
        loudness = loudness * jnp.repeat(draws, dims[dim] // shards_of).reshape([-1 if axis == dim else 1 for axis in range(len(dims))])
    return loudness


def gaussian(key, extent, width, reach, pieces=(), kind=jnp.bfloat16):
    loudness = level_of(key, extent, pieces, -0.22, 0.18) if pieces else 1.0
    result = jax.random.normal(key, extent, jnp.float32) * width * loudness
    return jnp.minimum(jnp.maximum(result, -reach), reach).astype(kind)


def setup_inputs(seed: int = 0) -> dict:
    seeds = jax.random.split(jax.random.key(seed), 4)
    return {
        "fields": gaussian(seeds[0], (4, NX, NY, NZ), 1.0, 4.0, ((1, 64), (2, 4)), jnp.float32),
        "embers": jnp.clip(0.05 + 0.95 * jax.random.uniform(seeds[1], (7, TD, TC, SLOTS, CAP), jnp.float32) ** level_of(seeds[1], (7, TD, TC, SLOTS, CAP), ((1, 64), (2, 4)), -0.2, 0.2), 0.05, 1.0),
        "counts": draw_counts(jax.random.fold_in(seeds[3], 71), 0),
    }


HORIZONTAL_MIX = 0.1
VERTICAL_MIX = 0.1
ADVECTION = 0.25
DRAG_RATE = 0.6
BURN_RATE = 0.5
HEAT_YIELD = 4.0
DESTINATIONS = ((1, -1), (1, 0), (1, 1), (2, -1), (2, 0), (2, 1))


def advance(padded):
    centre = padded[:, 1:-1, 1:-1]
    eastern = padded[:, 2:, 1:-1]
    western = padded[:, :-2, 1:-1]
    northern = padded[:, 1:-1, 2:]
    southern = padded[:, 1:-1, :-2]
    upper_level = jnp.concatenate([centre[..., 1:], centre[..., -1:]], axis=-1)
    lower_level = jnp.concatenate([centre[..., :1], centre[..., :-1]], axis=-1)
    spread = eastern + western + northern + southern - 4.0 * centre
    column_mix = upper_level + lower_level - 2.0 * centre
    carried = centre[0:1] * (eastern - western) * 0.5 + centre[1:2] * (northern - southern) * 0.5
    return centre + HORIZONTAL_MIX * spread + VERTICAL_MIX * column_mix - ADVECTION * carried


def tent_weights(position, cell_count):
    centres = jnp.arange(cell_count).astype(jnp.float32) + 0.5
    return jnp.maximum(0.0, 1.0 - jnp.abs(position[:, None] - centres[None, :]))


def ember_update(tile_fields, records):
    cells_down = tile_fields.shape[1]
    cells_cross = tile_fields.shape[2]
    levels = tile_fields.shape[3]
    weight_down = tent_weights(records[0] * cells_down, cells_down)
    weight_cross = tent_weights(records[1] * cells_cross, cells_cross)
    weight_level = tent_weights(records[2] * levels, levels)
    column = jnp.einsum("kxyz,ez->kxye", tile_fields, weight_level, precision=lax.Precision.HIGHEST)
    across = jnp.sum(column * weight_cross.T[None, None], axis=2)
    sampled = jnp.sum(across * weight_down.T[None], axis=1)
    ember_mass = records[5]
    burned = ember_mass * BURN_RATE * jax.nn.sigmoid(records[6] + sampled[2] - sampled[3])
    living = (ember_mass > 0.0).astype(tile_fields.dtype)
    landed = jnp.stack([
        records[3] + DRAG_RATE * (sampled[0] - records[3]),
        records[4] + DRAG_RATE * (sampled[1] - records[4]),
        records[6] + DRAG_RATE * (sampled[2] - records[6]),
        ember_mass - burned,
    ]) * living[None]
    spread = weight_down[:, :, None] * weight_cross[:, None, :] * (HEAT_YIELD * burned)[:, None, None]
    spread = spread.reshape(records.shape[1], cells_down * cells_cross)
    deposit = jnp.dot(spread.T, weight_level, precision=lax.Precision.HIGHEST)
    return landed, deposit.reshape(cells_down, cells_cross, levels)


def one_tile(tile_pair):
    return ember_update(tile_pair[0], tile_pair[1])


def reference(fields, embers, counts):
    slot_index = jnp.arange(CAP).astype(jnp.int32)
    live_mask = (slot_index[None, None, None, :] < counts[..., None]).astype(jnp.float32)
    outgoing = embers * live_mask[None]
    arrivals = []
    for target in range(SLOTS):
        down_step, cross_step = DESTINATIONS[target]
        shifted = outgoing[:, :, :, target]
        shifted = jnp.pad(shifted, ((0, 0), (down_step, 0), (0, 0), (0, 0)))[:, :TD]
        if cross_step > 0:
            shifted = jnp.pad(shifted, ((0, 0), (0, 0), (cross_step, 0), (0, 0)))[:, :, :TC]
        elif cross_step < 0:
            shifted = jnp.pad(shifted, ((0, 0), (0, 0), (0, -cross_step), (0, 0)))[:, :, -cross_step:]
        arrivals.append(shifted)
    arrived = jnp.stack(arrivals, axis=3)
    tile_fields = fields.reshape(4, TD, CX, TC, CY, NZ).transpose(1, 3, 0, 2, 4, 5).reshape(TD * TC, 4, CX, CY, NZ)
    tile_records = arrived.transpose(1, 2, 0, 3, 4).reshape(TD * TC, 7, SLOTS * CAP)
    landed, deposit = lax.map(one_tile, (tile_fields, tile_records))
    landed = landed.reshape(TD, TC, 4, SLOTS, CAP).transpose(2, 0, 1, 3, 4)
    deposit = deposit.reshape(TD, TC, CX, CY, NZ).transpose(0, 2, 1, 3, 4).reshape(NX, NY, NZ)
    current = fields
    for step_index in range(STEPS):
        padded = jnp.pad(current, ((0, 0), (1, 1), (1, 1), (0, 0)))
        current = advance(padded)
    advanced = jnp.concatenate([current[:2], current[2:3] + deposit[None], current[3:]], axis=0)
    return advanced, landed
```

```python
import jax
import jax.numpy as jnp
from jax import lax
from jax.experimental import pallas as pl
from jax.experimental.pallas import tpu as pltpu
from jax.sharding import PartitionSpec as P

STEPS = 6
HORIZONTAL_MIX = 0.1
VERTICAL_MIX = 0.1
ADVECTION = 0.25
DRAG_RATE = 0.6
BURN_RATE = 0.5
HEAT_YIELD = 4.0

CX, CY, NZ = 8, 64, 128
CAP = 256
H = STEPS
PAD = 16
WIDE = CY + 2 * PAD
TALL = CX + 2 * H
CORNER = ((1, 0, 5), (3, 5, 3), (2, 8, 4), (4, 12, 2), (5, 14, 1))
REC_ROWS = 24
E1_ROWS = REC_ROWS + 4 * 16
C_COLS = 0
C_CORN = 32
C_RECS = 48
C_ROWS = 52

VMEM = pl.BlockSpec(memory_space=pltpu.VMEM)
SMEM = pl.BlockSpec(memory_space=pltpu.SMEM)
ANY = pl.BlockSpec(memory_space=pl.ANY)


def pack_kernel(counts_ref, fields_ref, embers_ref, e1_ref, f1_ref, e2_ref):
    lane = lax.broadcasted_iota(jnp.int32, (1, CAP), 1)
    for slot in range(6):
        live = (lane < counts_ref[slot]).astype(jnp.float32)
        target = e1_ref if slot < 3 else e2_ref
        for comp in range(7):
            row = comp * 3 + slot % 3
            target[row : row + 1, :] = embers_ref[comp, slot : slot + 1, :] * live
    for k in range(4):
        for dist, first, cols in CORNER:
            at = REC_ROWS + 16 * k + first
            for ref, row in ((e1_ref, CX - dist), (f1_ref, dist - 1)):
                if ref is f1_ref:
                    at = 16 * k + first
                ref[at : at + cols, 0:NZ] = fields_ref[k, row, 0:cols, :]
                ref[at : at + cols, NZ:] = fields_ref[k, row, CY - cols : CY, :]
    zero = jnp.zeros((1, 2 * NZ), jnp.float32)
    for k in range(4):
        f1_ref[16 * k + 15 : 16 * k + 16, :] = zero
        e1_ref[REC_ROWS + 16 * k + 15 : REC_ROWS + 16 * k + 16, :] = zero
    e1_ref[21:24, :] = jnp.zeros((3, 2 * NZ), jnp.float32)
    e2_ref[21:24, :] = jnp.zeros((3, 2 * NZ), jnp.float32)


def turn_kernel(fields_ref, e1_ref, f1_ref, e2_ref, cp_ref, cm_ref):
    for out, side, slot in ((cp_ref, 1, 2), (cm_ref, 0, 0)):
        col = (CY - 8) * side
        for k in range(4):
            for row in range(CX):
                out[C_COLS + 8 * k + row] = fields_ref[k, row, col : col + 8, :]
            for half in range(2):
                at = 16 * k + 8 * half
                lanes = slice(NZ * side, NZ * side + NZ)
                out[C_CORN + 2 * k + half] = e1_ref[REC_ROWS + at : REC_ROWS + at + 8, lanes]
                out[C_CORN + 8 + 2 * k + half] = f1_ref[at : at + 8, lanes]
        for comp in range(7):
            for which, ref in ((0, e1_ref), (1, e2_ref)):
                for half in range(2):
                    row = (comp * 2 + which) * 2 + half
                    out[C_RECS + row // 8, row % 8 : row % 8 + 1, :] = ref[
                        comp * 3 + slot : comp * 3 + slot + 1, NZ * half : NZ * half + NZ
                    ]
        out[C_RECS + 3, 4:8, :] = jnp.zeros((4, NZ), jnp.float32)


def split(x):
    high = x.astype(jnp.bfloat16)
    low = (x - high.astype(jnp.float32)).astype(jnp.bfloat16)
    return high, low


def dot32(a, b):
    return lax.dot_general(a, b, (((1,), (0,)), ((), ())), preferred_element_type=jnp.float32)


def dot32t(a, b):
    return lax.dot_general(a, b, (((1,), (1,)), ((), ())), preferred_element_type=jnp.float32)


def tent(position, count):
    centre = lax.broadcasted_iota(jnp.int32, (count, CAP), 0).astype(jnp.float32) + 0.5
    return jnp.maximum(0.0, 1.0 - jnp.abs(position - centre))


def ember_kernel(
    fields_ref, e1_ref, e2_ref, cp_ref, cm_ref, landed_ref, deposit_ref, rec, parts, weight, fate
):
    cells = CX * CY
    for k in range(4):
        high, low = split(fields_ref[k].reshape(cells, NZ))
        parts[k, :, 0:NZ] = high
        parts[k, :, NZ:] = low
    deposit_ref[...] = jnp.zeros_like(deposit_ref)
    for comp in range(7):
        rec[1, comp : comp + 1, :] = e1_ref[comp * 3 + 1 : comp * 3 + 2, :]
        rec[4, comp : comp + 1, :] = e2_ref[comp * 3 + 1 : comp * 3 + 2, :]
        for which in range(2):
            for half in range(2):
                row = (comp * 2 + which) * 2 + half
                for ref, slot in ((cp_ref, 2), (cm_ref, 0)):
                    rec[3 * which + slot, comp : comp + 1, NZ * half : NZ * half + NZ] = ref[
                        C_RECS + row // 8, row % 8 : row % 8 + 1, :
                    ]

    @pl.loop(0, 6)
    def _(slot):
        field = [rec[slot, i : i + 1, :] for i in range(7)]
        down = tent(field[0] * CX, CX)
        cross = tent(field[1] * CY, CY)
        level = tent(field[2] * NZ, NZ)
        for x in range(CX):
            weight[CY * x : CY * x + CY, :] = down[x : x + 1, :] * cross
        level_high, level_low = split(level)
        both = jnp.concatenate([level_high, level_high], axis=0)
        sampled = []
        for k in range(4):
            column = dot32(parts[k], both) + dot32(parts[k, :, 0:NZ], level_low)
            sampled.append(jnp.sum(column * weight[...], axis=0, keepdims=True))
        mass = field[5]
        heat = field[6] + sampled[2] - sampled[3]
        burned = mass * BURN_RATE * jax.nn.sigmoid(heat)
        living = (mass > 0.0).astype(jnp.float32)
        fate[slot, 0:1, :] = (field[3] + DRAG_RATE * (sampled[0] - field[3])) * living
        fate[slot, 1:2, :] = (field[4] + DRAG_RATE * (sampled[1] - field[4])) * living
        fate[slot, 2:3, :] = (field[6] + DRAG_RATE * (sampled[2] - field[6])) * living
        fate[slot, 3:4, :] = (mass - burned) * living
        heat_high, heat_low = split(level * (HEAT_YIELD * burned))
        weight_high, weight_low = split(weight[...])
        extra = (
            dot32t(weight_high, heat_high)
            + dot32t(weight_high, heat_low)
            + dot32t(weight_low, heat_high)
        )
        deposit_ref[...] += extra

    for slot in range(6):
        for i in range(4):
            landed_ref[i, slot : slot + 1, :] = fate[slot, i : i + 1, :]


def stencil_kernel(
    flags_ref, up_ref, fields_ref, dn_ref, cp_ref, cm_ref, deposit_ref, out_ref, a, b, sems
):
    copies = [
        pltpu.make_async_copy(up_ref, a.at[:, 0:H, PAD : PAD + CY, :], sems.at[0]),
        pltpu.make_async_copy(fields_ref, a.at[:, H : H + CX, PAD : PAD + CY, :], sems.at[1]),
        pltpu.make_async_copy(dn_ref, a.at[:, H + CX :, PAD : PAD + CY, :], sems.at[2]),
    ]
    for copy in copies:
        copy.start()
    zero = jnp.zeros((PAD, NZ), jnp.float32)
    edge = jnp.zeros((8, NZ), jnp.float32)
    for k in range(4):
        for row in range(TALL):
            if H <= row < H + CX:
                a[k, row, 0:8, :] = edge
                a[k, row, 8:16, :] = cp_ref[C_COLS + 8 * k + row - H]
                a[k, row, PAD + CY : PAD + CY + 8, :] = cm_ref[C_COLS + 8 * k + row - H]
                a[k, row, PAD + CY + 8 :, :] = edge
            else:
                a[k, row, 0:PAD, :] = zero
                a[k, row, PAD + CY :, :] = zero
            b[k, row, 0:8, :] = edge
            b[k, row, PAD + CY + 8 :, :] = edge
        for dist, first, cols in CORNER:
            half, at = first // 8, first % 8
            for part, row in ((0, H - dist), (8, H + CX - 1 + dist)):
                entry = C_CORN + part + 2 * k + half
                a[k, row, PAD - cols : PAD, :] = cp_ref[entry, at : at + cols, :]
                a[k, row, PAD + CY : PAD + CY + cols, :] = cm_ref[entry, at : at + cols, :]
    for copy in copies:
        copy.wait()

    lane = lax.broadcasted_iota(jnp.int32, (8, NZ), 1)
    first_level = lane == 0
    last_level = lane == NZ - 1
    left, right = (flags_ref[2].astype(jnp.float32), flags_ref[3].astype(jnp.float32))

    def cell_block(src, row, col, scale):
        half_step = ADVECTION * 0.5 * scale
        mix = HORIZONTAL_MIX * scale
        u = src[0, row, col : col + 8, :] * half_step
        v = src[1, row, col : col + 8, :] * half_step
        east, west, north, south = (mix - u, mix + u, mix - v, mix + v)
        keep = (1.0 - 4.0 * HORIZONTAL_MIX - 2.0 * VERTICAL_MIX) * scale
        column = VERTICAL_MIX * scale
        out = []
        for k in range(4):
            f = src[k, row, col : col + 8, :]
            above = jnp.where(last_level, f, pltpu.roll(f, NZ - 1, 1))
            below = jnp.where(first_level, f, pltpu.roll(f, 1, 1))
            out.append(
                (keep * f + column * (above + below))
                + (east * src[k, row + 1, col : col + 8, :] + west * src[k, row - 1, col : col + 8, :])
                + (
                    north * src[k, row, col + 1 : col + 9, :]
                    + south * src[k, row, col - 1 : col + 7, :]
                )
            )
        return out

    for step in range(1, STEPS):
        src, dst = (a, b) if step % 2 == 1 else (b, a)

        @pl.loop(step, TALL - step)
        def _(row):
            inside = jnp.where(row < H, flags_ref[0], jnp.where(row >= H + CX, flags_ref[1], 1))
            inside = inside.astype(jnp.float32)
            for block in range(10):
                col = 8 + 8 * block
                scale = inside * left if block == 0 else inside * right if block == 9 else inside
                for k, value in enumerate(cell_block(src, row, col, scale)):
                    dst[k, row, col : col + 8, :] = value

    src = a if STEPS % 2 == 1 else b

    @pl.loop(0, CX)
    def _(row):
        for block in range(8):
            col = PAD + 8 * block
            for k, value in enumerate(cell_block(src, row + H, col, 1.0)):
                if k == 2:
                    value = value + deposit_ref[row, 8 * block : 8 * block + 8, :]
                out_ref[k, row, 8 * block : 8 * block + 8, :] = value


def struct(*shape):
    return jax.ShapeDtypeStruct(shape, jnp.float32)


def moved(x, axis, by):
    size = lax.axis_size(axis)
    pairs = [(i, i + by) for i in range(size) if 0 <= i + by < size]
    return lax.ppermute(x, axis, pairs)


PARAMS = pltpu.CompilerParams(vmem_limit_bytes=32 * 1024 * 1024)


def local(fields, embers, counts):
    down, cross = (lax.axis_index("down"), lax.axis_index("cross"))
    flags = jnp.stack(
        [
            down > 0,
            down < lax.axis_size("down") - 1,
            cross > 0,
            cross < lax.axis_size("cross") - 1,
        ]
    ).astype(jnp.int32)
    up = moved(fields[:, CX - H :], "down", 1)
    dn = moved(fields[:, :H], "down", -1)
    e1, f1, e2 = pl.pallas_call(
        pack_kernel,
        out_shape=(struct(E1_ROWS, CAP), struct(64, CAP), struct(REC_ROWS, CAP)),
        in_specs=[SMEM, VMEM, VMEM],
        out_specs=(VMEM, VMEM, VMEM),
        compiler_params=PARAMS,
        name="pack",
    )(counts[0, 0], fields, embers[:, 0, 0])
    e1 = moved(e1, "down", 1)
    f1 = moved(f1, "down", -1)
    e2 = moved(e2, "down", 2)
    cp, cm = pl.pallas_call(
        turn_kernel,
        out_shape=(struct(C_ROWS, 8, NZ), struct(C_ROWS, 8, NZ)),
        in_specs=[VMEM] * 4,
        out_specs=(VMEM, VMEM),
        compiler_params=PARAMS,
        name="turn",
    )(fields, e1, f1, e2)
    cp = moved(cp, "cross", 1)
    cm = moved(cm, "cross", -1)
    landed, deposit = pl.pallas_call(
        ember_kernel,
        out_shape=(struct(4, 6, CAP), struct(CX * CY, NZ)),
        in_specs=[VMEM] * 5,
        out_specs=(VMEM, VMEM),
        scratch_shapes=[
            pltpu.VMEM((6, 8, CAP), jnp.float32),
            pltpu.VMEM((4, CX * CY, 2 * NZ), jnp.bfloat16),
            pltpu.VMEM((CX * CY, CAP), jnp.float32),
            pltpu.VMEM((6, 8, CAP), jnp.float32),
        ],
        compiler_params=PARAMS,
        name="embers",
    )(fields, e1, e2, cp, cm)
    advanced = pl.pallas_call(
        stencil_kernel,
        out_shape=struct(4, CX, CY, NZ),
        in_specs=[SMEM, ANY, ANY, ANY, VMEM, VMEM, VMEM],
        out_specs=VMEM,
        scratch_shapes=[
            pltpu.VMEM((4, TALL, WIDE, NZ), jnp.float32),
            pltpu.VMEM((4, TALL, WIDE, NZ), jnp.float32),
            pltpu.SemaphoreType.DMA((3,)),
        ],
        compiler_params=PARAMS,
        name="stencil",
    )(flags, up, fields, dn, cp, cm, deposit.reshape(CX, CY, NZ))
    return (advanced, landed[:, None, None])


def solution(mesh):
    placed = (
        P(None, "down", "cross", None),
        P(None, "down", "cross", None, None),
        P("down", "cross", None),
    )
    return jax.shard_map(
        local,
        mesh=mesh,
        in_specs=placed,
        out_specs=(P(None, "down", "cross", None), P(None, "down", "cross", None, None)),
        check_vma=False,
    )
```

```python
import jax
import jax.numpy as jnp
from jax import lax
from jax.experimental import pallas as pl
from jax.experimental.pallas import tpu as pltpu
from jax.sharding import PartitionSpec as P

STEPS = 6
HORIZONTAL_MIX = 0.1
VERTICAL_MIX = 0.1
ADVECTION = 0.25
DRAG_RATE = 0.6
BURN_RATE = 0.5
HEAT_YIELD = 4.0

CX, CY, NZ = 8, 64, 128
CAP = 256
H = STEPS
NEAR = 3
FAR = H - NEAR
PAD = 16
WIDE = CY + 2 * PAD
TALL = CX + 2 * H
TOP = H - NEAR
CORNER = {1: 0, 3: 5, 2: 8, 4: 12, 5: 14}
E_CORN = 6
C_RECS = 32
C_BLOCKS = 36

HBM = pl.BlockSpec(memory_space=pltpu.HBM)
VMEM = pl.BlockSpec(memory_space=pltpu.VMEM)
SMEM = pl.BlockSpec(memory_space=pltpu.SMEM)
ANY = pl.BlockSpec(memory_space=pl.ANY)


def corner_entry(k, dist, side):
    return (2 * k + CORNER[dist] // 8) * 2 + side


def edge_kernel(
    counts_ref, embers_ref, fields_hbm, cp_ref, cm_ref, own_ref, fields_ref, counts, embers, sems
):
    copies = [
        pltpu.make_async_copy(counts_ref, counts, sems.at[0]),
        pltpu.make_async_copy(embers_ref, embers, sems.at[1]),
        pltpu.make_async_copy(fields_hbm, fields_ref, sems.at[2]),
    ]
    for copy in copies:
        copy.start()
    for copy in copies[:2]:
        copy.wait()
    lane = lax.broadcasted_iota(jnp.int32, (1, NZ), 1)
    for slot in range(6):
        base, target = ((C_RECS, cm_ref), (0, own_ref), (C_RECS, cp_ref))[slot % 3]
        for half in range(2):
            live = (lane + NZ * half < counts[0, 0, slot]).astype(jnp.float32)
            for comp in range(7):
                row = comp * 12 + slot * 2 + half
                put = comp * 4 + slot // 3 * 2 + half
                target[base + put // 8, put % 8 : put % 8 + 1, :] = (
                    embers[row // 4, row % 4 : row % 4 + 1, :] * live
                )
    for base, target in ((C_RECS, cm_ref), (0, own_ref), (C_RECS, cp_ref)):
        target[base + 3, 4:8, :] = jnp.zeros((4, NZ), jnp.float32)
    copies[2].wait()
    for k in range(4):
        for row in range(CX):
            cp_ref[8 * k + row] = fields_ref[k, row, CY - 8 :, :]
            cm_ref[8 * k + row] = fields_ref[k, row, 0:8, :]


def records_kernel(cp_ref, cm_ref, own_ref, e1_ref, f1_ref, e2_ref):
    for which, target in ((0, e1_ref), (1, e2_ref)):
        for j, base, ref in ((0, C_RECS, cm_ref), (1, 0, own_ref), (2, C_RECS, cp_ref)):
            for comp in range(7):
                for half in range(2):
                    row = comp * 4 + which * 2 + half
                    put = comp * 6 + j * 2 + half
                    target[put // 8, put % 8 : put % 8 + 1, :] = ref[
                        base + row // 8, row % 8 : row % 8 + 1, :
                    ]
        target[5, 2:8, :] = jnp.zeros((6, NZ), jnp.float32)
    for k in range(4):
        for ref, base, up in ((e1_ref, E_CORN, True), (f1_ref, 0, False)):
            for dist, first in CORNER.items():
                cols = H - dist
                at = first % 8
                row = CX - dist if up else dist - 1
                ref[base + corner_entry(k, dist, 0), at : at + cols, :] = cp_ref[
                    8 * k + row, 8 - cols : 8, :
                ]
                ref[base + corner_entry(k, dist, 1), at : at + cols, :] = cm_ref[
                    8 * k + row, 0:cols, :
                ]
            for side in range(2):
                ref[base + corner_entry(k, 5, side), 7:8, :] = jnp.zeros((1, NZ), jnp.float32)


def pack_kernel(fields_ref, ua_ref, da_ref, ub_ref, db_ref):
    for k in range(4):
        for i in range(NEAR):
            ua_ref[k, i] = fields_ref[k, CX - NEAR + i]
            da_ref[k, i] = fields_ref[k, i]
        for i in range(FAR):
            ub_ref[k, i] = fields_ref[k, CX - H + i]
            db_ref[k, i] = fields_ref[k, NEAR + i]


def split(x):
    high = x.astype(jnp.bfloat16)
    low = (x - high.astype(jnp.float32)).astype(jnp.bfloat16)
    return high, low


def dot32(a, b):
    return lax.dot_general(a, b, (((1,), (0,)), ((), ())), preferred_element_type=jnp.float32)


def dot32t(a, b):
    return lax.dot_general(a, b, (((1,), (1,)), ((), ())), preferred_element_type=jnp.float32)


def tent(position, count):
    centre = lax.broadcasted_iota(jnp.int32, (count, CAP), 0).astype(jnp.float32) + 0.5
    return jnp.maximum(0.0, 1.0 - jnp.abs(position - centre))


def ember_kernel(
    fields_ref, e1_ref, e2_ref, landed_ref, deposit_ref, rec, parts, weight, fate
):
    cells = CX * CY
    for k in range(4):
        high, low = split(fields_ref[k].reshape(cells, NZ))
        parts[k, :, 0:NZ] = high
        parts[k, :, NZ:] = low
    deposit_ref[...] = jnp.zeros_like(deposit_ref)
    for slot in range(6):
        ref = e1_ref if slot < 3 else e2_ref
        for comp in range(7):
            for half in range(2):
                row = comp * 6 + slot % 3 * 2 + half
                rec[slot, comp : comp + 1, NZ * half : NZ * half + NZ] = ref[
                    row // 8, row % 8 : row % 8 + 1, :
                ]

    @pl.loop(0, 6)
    def _(slot):
        field = [rec[slot, i : i + 1, :] for i in range(7)]
        down = tent(field[0] * CX, CX)
        cross = tent(field[1] * CY, CY)
        level = tent(field[2] * NZ, NZ)
        for x in range(CX):
            weight[CY * x : CY * x + CY, :] = down[x : x + 1, :] * cross
        level_high, level_low = split(level)
        both = jnp.concatenate([level_high, level_high], axis=0)
        sampled = []
        for k in range(4):
            column = dot32(parts[k], both) + dot32(parts[k, :, 0:NZ], level_low)
            sampled.append(jnp.sum(column * weight[...], axis=0, keepdims=True))
        mass = field[5]
        heat = field[6] + sampled[2] - sampled[3]
        burned = mass * BURN_RATE * jax.nn.sigmoid(heat)
        living = (mass > 0.0).astype(jnp.float32)
        fate[slot, 0:1, :] = (field[3] + DRAG_RATE * (sampled[0] - field[3])) * living
        fate[slot, 1:2, :] = (field[4] + DRAG_RATE * (sampled[1] - field[4])) * living
        fate[slot, 2:3, :] = (field[6] + DRAG_RATE * (sampled[2] - field[6])) * living
        fate[slot, 3:4, :] = (mass - burned) * living
        heat_high, heat_low = split(level * (HEAT_YIELD * burned))
        weight_high, weight_low = split(weight[...])
        extra = (
            dot32t(weight_high, heat_high)
            + dot32t(weight_high, heat_low)
            + dot32t(weight_low, heat_high)
        )
        deposit_ref[...] += extra

    for slot in range(6):
        for i in range(4):
            for half in range(2):
                row = i * 12 + slot * 2 + half
                landed_ref[row // 4, row % 4 : row % 4 + 1, :] = fate[
                    slot, i : i + 1, NZ * half : NZ * half + NZ
                ]


def edges():
    lane = lax.broadcasted_iota(jnp.int32, (8, NZ), 1)
    return lane == 0, lane == NZ - 1


def cell_block(src, row, col, scale, ends):
    first_level, last_level = ends
    half_step = ADVECTION * 0.5 * scale
    mix = HORIZONTAL_MIX * scale
    u = src[0, row, col : col + 8, :] * half_step
    v = src[1, row, col : col + 8, :] * half_step
    east, west, north, south = (mix - u, mix + u, mix - v, mix + v)
    keep = (1.0 - 4.0 * HORIZONTAL_MIX - 2.0 * VERTICAL_MIX) * scale
    column = VERTICAL_MIX * scale
    out = []
    for k in range(4):
        f = src[k, row, col : col + 8, :]
        above = jnp.where(last_level, f, pltpu.roll(f, NZ - 1, 1))
        below = jnp.where(first_level, f, pltpu.roll(f, 1, 1))
        out.append(
            (keep * f + column * (above + below))
            + (east * src[k, row + 1, col : col + 8, :] + west * src[k, row - 1, col : col + 8, :])
            + (
                north * src[k, row, col + 1 : col + 9, :]
                + south * src[k, row, col - 1 : col + 7, :]
            )
        )
    return out


def wide_row(flags_ref, src, dst, row, ends):
    inside = jnp.where(row < H, flags_ref[0], jnp.where(row >= H + CX, flags_ref[1], 1))
    inside = inside.astype(jnp.float32)
    left, right = (flags_ref[2].astype(jnp.float32), flags_ref[3].astype(jnp.float32))
    for block in range(10):
        col = 8 + 8 * block
        scale = inside * left if block == 0 else inside * right if block == 9 else inside
        for k, value in enumerate(cell_block(src, row, col, scale, ends)):
            dst[k, row, col : col + 8, :] = value


def fill_sides(a, rows, e1_ref, f1_ref):
    zero = jnp.zeros((PAD, NZ), jnp.float32)
    for k in range(4):
        for row in rows:
            a[k, row, 0:PAD, :] = zero
            a[k, row, PAD + CY :, :] = zero
            ref, base, dist = (e1_ref, E_CORN, H - row)
            if row >= H:
                ref, base, dist = (f1_ref, 0, row - (H + CX - 1))
            if dist in CORNER:
                cols, at = H - dist, CORNER[dist] % 8
                a[k, row, PAD - cols : PAD, :] = ref[
                    base + corner_entry(k, dist, 0), at : at + cols, :
                ]
                a[k, row, PAD + CY : PAD + CY + cols, :] = ref[
                    base + corner_entry(k, dist, 1), at : at + cols, :
                ]


def near_kernel(
    flags_ref, fields_ref, ua_ref, da_ref, cp_ref, cm_ref, e1_ref, f1_ref, a, b, sem
):
    copy = pltpu.make_async_copy(fields_ref, a.at[:, H : H + CX, PAD : PAD + CY, :], sem)
    copy.start()
    edge = jnp.zeros((8, NZ), jnp.float32)
    for k in range(4):
        for row in range(CX):
            a[k, H + row, 0:8, :] = edge
            a[k, H + row, 8:16, :] = cp_ref[8 * k + row]
            a[k, H + row, PAD + CY : PAD + CY + 8, :] = cm_ref[8 * k + row]
            a[k, H + row, PAD + CY + 8 :, :] = edge
        for i in range(NEAR):
            a[k, TOP + i, PAD : PAD + CY, :] = ua_ref[k, i]
            a[k, H + CX + i, PAD : PAD + CY, :] = da_ref[k, i]
        for row in range(TALL):
            b[k, row, 0:8, :] = edge
            b[k, row, PAD + CY + 8 :, :] = edge
    fill_sides(a, (*range(TOP, H), *range(H + CX, H + CX + NEAR)), e1_ref, f1_ref)
    copy.wait()
    ends = edges()
    for step in range(1, STEPS + 1):
        src, dst = (a, b) if step % 2 == 1 else (b, a)
        if TOP + step < TALL - TOP - step:

            @pl.loop(TOP + step, TALL - TOP - step)
            def _(row):
                wide_row(flags_ref, src, dst, row, ends)


def far_kernel(
    flags_ref, ub_ref, db_ref, e1_ref, f1_ref, deposit_ref, a_in, b_in, out_ref, a, b
):
    fill_sides(a, (*range(FAR), *range(TALL - FAR, TALL)), e1_ref, f1_ref)
    for k in range(4):
        for i in range(FAR):
            a[k, i, PAD : PAD + CY, :] = ub_ref[k, i]
            a[k, TALL - FAR + i, PAD : PAD + CY, :] = db_ref[k, i]
    ends = edges()
    for step in range(1, STEPS):
        src, dst = (a, b) if step % 2 == 1 else (b, a)

        @pl.loop(0, FAR)
        def _(i):
            wide_row(flags_ref, src, dst, i + step, ends)
            wide_row(flags_ref, src, dst, TALL - 1 - step - i, ends)

    src, dst = (a, b) if STEPS % 2 == 1 else (b, a)

    def last_row(row, values):
        for block in range(8):
            for k, value in enumerate(values(row, PAD + 8 * block)):
                if k == 2:
                    value = value + deposit_ref[row, 8 * block : 8 * block + 8, :]
                out_ref[k, row, 8 * block : 8 * block + 8, :] = value

    def computed(row, col):
        return cell_block(src, row + H, col, 1.0, ends)

    def kept(row, col):
        return [dst[k, row + H, col : col + 8, :] for k in range(4)]

    done = range(H - NEAR, NEAR + CX - H)
    if len(done):

        @pl.loop(0, done.start)
        def _(row):
            last_row(row, computed)
            last_row(CX - 1 - row, computed)

        for row in done:
            last_row(row, kept)
    else:

        @pl.loop(0, CX)
        def _(row):
            last_row(row, computed)


def struct(*shape):
    return jax.ShapeDtypeStruct(shape, jnp.float32)


def moved(x, axis, by):
    size = lax.axis_size(axis)
    pairs = [(i, i + by) for i in range(size) if 0 <= i + by < size]
    return lax.ppermute(x, axis, pairs)


PARAMS = pltpu.CompilerParams(vmem_limit_bytes=32 * 1024 * 1024)


def local(fields, embers, counts):
    down, cross = (lax.axis_index("down"), lax.axis_index("cross"))
    flags = jnp.stack(
        [
            down > 0,
            down < lax.axis_size("down") - 1,
            cross > 0,
            cross < lax.axis_size("cross") - 1,
        ]
    ).astype(jnp.int32)
    cp, cm, own, fields = pl.pallas_call(
        edge_kernel,
        out_shape=(
            struct(C_BLOCKS, 8, NZ),
            struct(C_BLOCKS, 8, NZ),
            struct(4, 8, NZ),
            struct(4, CX, CY, NZ),
        ),
        in_specs=[HBM, HBM, HBM],
        out_specs=(VMEM,) * 4,
        scratch_shapes=[
            pltpu.SMEM((1, 1, 6), jnp.int32),
            pltpu.VMEM((21, 4, NZ), jnp.float32),
            pltpu.SemaphoreType.DMA((3,)),
        ],
        compiler_params=PARAMS,
        name="edges",
    )(counts, embers.reshape(21, 4, NZ), fields)
    cp = moved(cp, "cross", 1)
    cm = moved(cm, "cross", -1)
    ua, da, ub, db = pl.pallas_call(
        pack_kernel,
        out_shape=(
            struct(4, NEAR, CY, NZ),
            struct(4, NEAR, CY, NZ),
            struct(4, FAR, CY, NZ),
            struct(4, FAR, CY, NZ),
        ),
        in_specs=[VMEM],
        out_specs=(VMEM,) * 4,
        compiler_params=PARAMS,
        name="pack",
    )(fields)
    ua = moved(ua, "down", 1)
    da = moved(da, "down", -1)
    e1, f1, e2 = pl.pallas_call(
        records_kernel,
        out_shape=(struct(E_CORN + 16, 8, NZ), struct(16, 8, NZ), struct(6, 8, NZ)),
        in_specs=[VMEM] * 3,
        out_specs=(VMEM,) * 3,
        compiler_params=PARAMS,
        name="records",
    )(cp, cm, own)
    e1 = moved(e1, "down", 1)
    f1 = moved(f1, "down", -1)
    e2 = moved(e2, "down", 2)
    ub, db, e1, f1, e2 = lax.optimization_barrier((ub, db, e1, f1, e2))
    ub = moved(ub, "down", 1)
    db = moved(db, "down", -1)
    landed, deposit = pl.pallas_call(
        ember_kernel,
        out_shape=(struct(12, 4, NZ), struct(CX * CY, NZ)),
        in_specs=[VMEM] * 3,
        out_specs=(VMEM, VMEM),
        scratch_shapes=[
            pltpu.VMEM((6, 8, CAP), jnp.float32),
            pltpu.VMEM((4, CX * CY, 2 * NZ), jnp.bfloat16),
            pltpu.VMEM((CX * CY, CAP), jnp.float32),
            pltpu.VMEM((6, 8, CAP), jnp.float32),
        ],
        compiler_params=PARAMS,
        name="embers",
    )(fields, e1, e2)
    tile = struct(4, TALL, WIDE, NZ)
    a, b = pl.pallas_call(
        near_kernel,
        out_shape=(tile, tile),
        in_specs=[SMEM, ANY] + [VMEM] * 6,
        out_specs=(VMEM, VMEM),
        scratch_shapes=[pltpu.SemaphoreType.DMA],
        compiler_params=PARAMS,
        name="near",
    )(flags, fields, ua, da, cp, cm, e1, f1)
    advanced, _, _ = pl.pallas_call(
        far_kernel,
        out_shape=(struct(4, CX, CY, NZ), tile, tile),
        in_specs=[SMEM] + [VMEM] * 7,
        out_specs=(VMEM, VMEM, VMEM),
        input_output_aliases={6: 1, 7: 2},
        compiler_params=PARAMS,
        name="far",
    )(flags, ub, db, e1, f1, deposit.reshape(CX, CY, NZ), a, b)
    return (advanced, landed.reshape(4, 1, 1, 6, CAP))


def solution(mesh):
    placed = (
        P(None, "down", "cross", None),
        P(None, "down", "cross", None, None),
        P("down", "cross", None),
    )
    return jax.shard_map(
        local,
        mesh=mesh,
        in_specs=placed,
        out_specs=(P(None, "down", "cross", None), P(None, "down", "cross", None, None)),
        check_vma=False,
    )
```

```python
import jax
import jax.numpy as jnp
from jax import lax
from jax.experimental import pallas as pl
from jax.experimental.pallas import tpu as pltpu
from jax.sharding import PartitionSpec as P

STEPS = 6
HORIZONTAL_MIX = 0.1
VERTICAL_MIX = 0.1
ADVECTION = 0.25
DRAG_RATE = 0.6
BURN_RATE = 0.5
HEAT_YIELD = 4.0

CX, CY, NZ = 8, 64, 128
CAP = 256
H = STEPS
NEAR = 3
FAR = H - NEAR
PAD = 16
WIDE = CY + 2 * PAD
TALL = CX + 2 * H
TOP = H - NEAR
CORNER = {1: 0, 3: 5, 2: 8, 4: 12, 5: 14}
B_CORN = 32 * NEAR
A_BLOCKS = B_CORN + 16
C_RECS = 32
C_BLOCKS = 36

HBM = pl.BlockSpec(memory_space=pltpu.HBM)
VMEM = pl.BlockSpec(memory_space=pltpu.VMEM)
SMEM = pl.BlockSpec(memory_space=pltpu.SMEM)
ANY = pl.BlockSpec(memory_space=pl.ANY)


def corner_entry(k, dist, side):
    return B_CORN + (2 * k + CORNER[dist] // 8) * 2 + side


def edge_kernel(
    counts_ref, embers_ref, fields_hbm, cp_ref, cm_ref, own_ref, fields_ref, counts, embers, sems
):
    copies = [
        pltpu.make_async_copy(counts_ref, counts, sems.at[0]),
        pltpu.make_async_copy(embers_ref, embers, sems.at[1]),
        pltpu.make_async_copy(fields_hbm, fields_ref, sems.at[2]),
    ]
    for copy in copies:
        copy.start()
    for copy in copies[:2]:
        copy.wait()
    lane = lax.broadcasted_iota(jnp.int32, (1, NZ), 1)
    for slot in range(6):
        base, target = ((C_RECS, cm_ref), (0, own_ref), (C_RECS, cp_ref))[slot % 3]
        for half in range(2):
            live = (lane + NZ * half < counts[0, 0, slot]).astype(jnp.float32)
            for comp in range(7):
                row = comp * 12 + slot * 2 + half
                put = comp * 4 + slot // 3 * 2 + half
                target[base + put // 8, put % 8 : put % 8 + 1, :] = (
                    embers[row // 4, row % 4 : row % 4 + 1, :] * live
                )
    for base, target in ((C_RECS, cm_ref), (0, own_ref), (C_RECS, cp_ref)):
        target[base + 3, 4:8, :] = jnp.zeros((4, NZ), jnp.float32)
    copies[2].wait()
    for k in range(4):
        for row in range(CX):
            cp_ref[8 * k + row] = fields_ref[k, row, CY - 8 :, :]
            cm_ref[8 * k + row] = fields_ref[k, row, 0:8, :]


def records_kernel(cp_ref, cm_ref, own_ref, e1_ref, e2_ref):
    for which, target in ((0, e1_ref), (1, e2_ref)):
        for j, base, ref in ((0, C_RECS, cm_ref), (1, 0, own_ref), (2, C_RECS, cp_ref)):
            for comp in range(7):
                for half in range(2):
                    row = comp * 4 + which * 2 + half
                    put = comp * 6 + j * 2 + half
                    target[put // 8, put % 8 : put % 8 + 1, :] = ref[
                        base + row // 8, row % 8 : row % 8 + 1, :
                    ]
        target[5, 2:8, :] = jnp.zeros((6, NZ), jnp.float32)


def pack_kernel(fields_ref, cp_ref, cm_ref, ua_ref, da_ref, ub_ref, db_ref):
    for k in range(4):
        for i in range(NEAR):
            for j in range(8):
                at = (k * NEAR + i) * 8 + j
                ua_ref[at] = fields_ref[k, CX - NEAR + i, 8 * j : 8 * j + 8, :]
                da_ref[at] = fields_ref[k, i, 8 * j : 8 * j + 8, :]
        for ref, up in ((ua_ref, True), (da_ref, False)):
            for dist, first in CORNER.items():
                cols = H - dist
                at = first % 8
                row = CX - dist if up else dist - 1
                ref[corner_entry(k, dist, 0), at : at + cols, :] = cp_ref[
                    8 * k + row, 8 - cols : 8, :
                ]
                ref[corner_entry(k, dist, 1), at : at + cols, :] = cm_ref[8 * k + row, 0:cols, :]
            for side in range(2):
                ref[corner_entry(k, 5, side), 7:8, :] = jnp.zeros((1, NZ), jnp.float32)
        for i in range(FAR):
            ub_ref[k, i] = fields_ref[k, CX - H + i]
            db_ref[k, i] = fields_ref[k, NEAR + i]


def split(x):
    high = x.astype(jnp.bfloat16)
    low = (x - high.astype(jnp.float32)).astype(jnp.bfloat16)
    return high, low


def dot32(a, b):
    return lax.dot_general(a, b, (((1,), (0,)), ((), ())), preferred_element_type=jnp.float32)


def dot32t(a, b):
    return lax.dot_general(a, b, (((1,), (1,)), ((), ())), preferred_element_type=jnp.float32)


def tent(position, count):
    centre = lax.broadcasted_iota(jnp.int32, (count, CAP), 0).astype(jnp.float32) + 0.5
    return jnp.maximum(0.0, 1.0 - jnp.abs(position - centre))


def ember_kernel(
    fields_ref, e1_ref, e2_ref, landed_ref, deposit_ref, rec, parts, weight, fate
):
    cells = CX * CY
    for k in range(4):
        high, low = split(fields_ref[k].reshape(cells, NZ))
        parts[k, :, 0:NZ] = high
        parts[k, :, NZ:] = low
    deposit_ref[...] = jnp.zeros_like(deposit_ref)
    for slot in range(6):
        ref = e1_ref if slot < 3 else e2_ref
        for comp in range(7):
            for half in range(2):
                row = comp * 6 + slot % 3 * 2 + half
                rec[slot, comp : comp + 1, NZ * half : NZ * half + NZ] = ref[
                    row // 8, row % 8 : row % 8 + 1, :
                ]

    @pl.loop(0, 6)
    def _(slot):
        field = [rec[slot, i : i + 1, :] for i in range(7)]
        down = tent(field[0] * CX, CX)
        cross = tent(field[1] * CY, CY)
        level = tent(field[2] * NZ, NZ)
        for x in range(CX):
            weight[CY * x : CY * x + CY, :] = down[x : x + 1, :] * cross
        level_high, level_low = split(level)
        both = jnp.concatenate([level_high, level_high], axis=0)
        sampled = []
        for k in range(4):
            column = dot32(parts[k], both) + dot32(parts[k, :, 0:NZ], level_low)
            sampled.append(jnp.sum(column * weight[...], axis=0, keepdims=True))
        mass = field[5]
        heat = field[6] + sampled[2] - sampled[3]
        burned = mass * BURN_RATE * jax.nn.sigmoid(heat)
        living = (mass > 0.0).astype(jnp.float32)
        fate[slot, 0:1, :] = (field[3] + DRAG_RATE * (sampled[0] - field[3])) * living
        fate[slot, 1:2, :] = (field[4] + DRAG_RATE * (sampled[1] - field[4])) * living
        fate[slot, 2:3, :] = (field[6] + DRAG_RATE * (sampled[2] - field[6])) * living
        fate[slot, 3:4, :] = (mass - burned) * living
        heat_high, heat_low = split(level * (HEAT_YIELD * burned))
        weight_high, weight_low = split(weight[...])
        extra = (
            dot32t(weight_high, heat_high)
            + dot32t(weight_high, heat_low)
            + dot32t(weight_low, heat_high)
        )
        deposit_ref[...] += extra

    for slot in range(6):
        for i in range(4):
            for half in range(2):
                row = i * 12 + slot * 2 + half
                landed_ref[row // 4, row % 4 : row % 4 + 1, :] = fate[
                    slot, i : i + 1, NZ * half : NZ * half + NZ
                ]


def edges():
    lane = lax.broadcasted_iota(jnp.int32, (8, NZ), 1)
    return lane == 0, lane == NZ - 1


def cell_block(src, row, col, scale, ends):
    first_level, last_level = ends
    half_step = ADVECTION * 0.5 * scale
    mix = HORIZONTAL_MIX * scale
    u = src[0, row, col : col + 8, :] * half_step
    v = src[1, row, col : col + 8, :] * half_step
    east, west, north, south = (mix - u, mix + u, mix - v, mix + v)
    keep = (1.0 - 4.0 * HORIZONTAL_MIX - 2.0 * VERTICAL_MIX) * scale
    column = VERTICAL_MIX * scale
    out = []
    for k in range(4):
        f = src[k, row, col : col + 8, :]
        above = jnp.where(last_level, f, pltpu.roll(f, NZ - 1, 1))
        below = jnp.where(first_level, f, pltpu.roll(f, 1, 1))
        out.append(
            (keep * f + column * (above + below))
            + (east * src[k, row + 1, col : col + 8, :] + west * src[k, row - 1, col : col + 8, :])
            + (
                north * src[k, row, col + 1 : col + 9, :]
                + south * src[k, row, col - 1 : col + 7, :]
            )
        )
    return out


def wide_row(flags_ref, src, dst, row, ends):
    inside = jnp.where(row < H, flags_ref[0], jnp.where(row >= H + CX, flags_ref[1], 1))
    inside = inside.astype(jnp.float32)
    left, right = (flags_ref[2].astype(jnp.float32), flags_ref[3].astype(jnp.float32))
    for block in range(10):
        col = 8 + 8 * block
        scale = inside * left if block == 0 else inside * right if block == 9 else inside
        for k, value in enumerate(cell_block(src, row, col, scale, ends)):
            dst[k, row, col : col + 8, :] = value


def fill_sides(a, rows, ua_ref, da_ref):
    zero = jnp.zeros((PAD, NZ), jnp.float32)
    for k in range(4):
        for row in rows:
            a[k, row, 0:PAD, :] = zero
            a[k, row, PAD + CY :, :] = zero
            ref, dist = (ua_ref, H - row) if row < H else (da_ref, row - (H + CX - 1))
            if dist in CORNER:
                cols, at = H - dist, CORNER[dist] % 8
                a[k, row, PAD - cols : PAD, :] = ref[corner_entry(k, dist, 0), at : at + cols, :]
                a[k, row, PAD + CY : PAD + CY + cols, :] = ref[
                    corner_entry(k, dist, 1), at : at + cols, :
                ]


def near_kernel(flags_ref, fields_ref, ua_ref, da_ref, cp_ref, cm_ref, a, b, sem):
    copy = pltpu.make_async_copy(fields_ref, a.at[:, H : H + CX, PAD : PAD + CY, :], sem)
    copy.start()
    edge = jnp.zeros((8, NZ), jnp.float32)
    for k in range(4):
        for row in range(CX):
            a[k, H + row, 0:8, :] = edge
            a[k, H + row, 8:16, :] = cp_ref[8 * k + row]
            a[k, H + row, PAD + CY : PAD + CY + 8, :] = cm_ref[8 * k + row]
            a[k, H + row, PAD + CY + 8 :, :] = edge
        for i in range(NEAR):
            for j in range(8):
                at = (k * NEAR + i) * 8 + j
                a[k, TOP + i, PAD + 8 * j : PAD + 8 * j + 8, :] = ua_ref[at]
                a[k, H + CX + i, PAD + 8 * j : PAD + 8 * j + 8, :] = da_ref[at]
        for row in range(TALL):
            b[k, row, 0:8, :] = edge
            b[k, row, PAD + CY + 8 :, :] = edge
    fill_sides(a, (*range(TOP, H), *range(H + CX, H + CX + NEAR)), ua_ref, da_ref)
    copy.wait()
    ends = edges()
    for step in range(1, STEPS + 1):
        src, dst = (a, b) if step % 2 == 1 else (b, a)
        if TOP + step < TALL - TOP - step:

            @pl.loop(TOP + step, TALL - TOP - step)
            def _(row):
                wide_row(flags_ref, src, dst, row, ends)


def far_kernel(
    flags_ref, ub_ref, db_ref, ua_ref, da_ref, deposit_ref, a_in, b_in, out_ref, a, b
):
    fill_sides(a, (*range(FAR), *range(TALL - FAR, TALL)), ua_ref, da_ref)
    for k in range(4):
        for i in range(FAR):
            a[k, i, PAD : PAD + CY, :] = ub_ref[k, i]
            a[k, TALL - FAR + i, PAD : PAD + CY, :] = db_ref[k, i]
    ends = edges()
    for step in range(1, STEPS):
        src, dst = (a, b) if step % 2 == 1 else (b, a)

        @pl.loop(0, FAR)
        def _(i):
            wide_row(flags_ref, src, dst, i + step, ends)
            wide_row(flags_ref, src, dst, TALL - 1 - step - i, ends)

    src, dst = (a, b) if STEPS % 2 == 1 else (b, a)

    def last_row(row, values):
        for block in range(8):
            for k, value in enumerate(values(row, PAD + 8 * block)):
                if k == 2:
                    value = value + deposit_ref[row, 8 * block : 8 * block + 8, :]
                out_ref[k, row, 8 * block : 8 * block + 8, :] = value

    def computed(row, col):
        return cell_block(src, row + H, col, 1.0, ends)

    def kept(row, col):
        return [dst[k, row + H, col : col + 8, :] for k in range(4)]

    done = range(H - NEAR, NEAR + CX - H)
    if len(done):

        @pl.loop(0, done.start)
        def _(row):
            last_row(row, computed)
            last_row(CX - 1 - row, computed)

        for row in done:
            last_row(row, kept)
    else:

        @pl.loop(0, CX)
        def _(row):
            last_row(row, computed)


def struct(*shape):
    return jax.ShapeDtypeStruct(shape, jnp.float32)


def moved(x, axis, by):
    size = lax.axis_size(axis)
    pairs = [(i, i + by) for i in range(size) if 0 <= i + by < size]
    return lax.ppermute(x, axis, pairs)


PARAMS = pltpu.CompilerParams(vmem_limit_bytes=32 * 1024 * 1024)


def local(fields, embers, counts):
    down, cross = (lax.axis_index("down"), lax.axis_index("cross"))
    flags = jnp.stack(
        [
            down > 0,
            down < lax.axis_size("down") - 1,
            cross > 0,
            cross < lax.axis_size("cross") - 1,
        ]
    ).astype(jnp.int32)
    cp, cm, own, fields = pl.pallas_call(
        edge_kernel,
        out_shape=(
            struct(C_BLOCKS, 8, NZ),
            struct(C_BLOCKS, 8, NZ),
            struct(4, 8, NZ),
            struct(4, CX, CY, NZ),
        ),
        in_specs=[HBM, HBM, HBM],
        out_specs=(VMEM,) * 4,
        scratch_shapes=[
            pltpu.SMEM((1, 1, 6), jnp.int32),
            pltpu.VMEM((21, 4, NZ), jnp.float32),
            pltpu.SemaphoreType.DMA((3,)),
        ],
        compiler_params=PARAMS,
        name="edges",
    )(counts, embers.reshape(21, 4, NZ), fields)
    cp = moved(cp, "cross", 1)
    cm = moved(cm, "cross", -1)
    e1, e2 = pl.pallas_call(
        records_kernel,
        out_shape=(struct(6, 8, NZ), struct(6, 8, NZ)),
        in_specs=[VMEM] * 3,
        out_specs=(VMEM, VMEM),
        compiler_params=PARAMS,
        name="records",
    )(cp, cm, own)
    e1 = moved(e1, "down", 1)
    e2 = moved(e2, "down", 2)
    ua, da, ub, db = pl.pallas_call(
        pack_kernel,
        out_shape=(
            struct(A_BLOCKS, 8, NZ),
            struct(A_BLOCKS, 8, NZ),
            struct(4, FAR, CY, NZ),
            struct(4, FAR, CY, NZ),
        ),
        in_specs=[VMEM] * 3,
        out_specs=(VMEM,) * 4,
        compiler_params=PARAMS,
        name="pack",
    )(fields, cp, cm)
    ua = moved(ua, "down", 1)
    da = moved(da, "down", -1)
    ub = moved(ub, "down", 1)
    db = moved(db, "down", -1)
    tile = struct(4, TALL, WIDE, NZ)
    a, b = pl.pallas_call(
        near_kernel,
        out_shape=(tile, tile),
        in_specs=[SMEM, ANY, VMEM, VMEM, VMEM, VMEM],
        out_specs=(VMEM, VMEM),
        scratch_shapes=[pltpu.SemaphoreType.DMA],
        compiler_params=PARAMS,
        cost_estimate=pl.CostEstimate(flops=1_000_000_000, bytes_accessed=0, transcendentals=0),
        name="near",
    )(flags, fields, ua, da, cp, cm)
    a, b, e1, e2 = lax.optimization_barrier((a, b, e1, e2))
    landed, deposit = pl.pallas_call(
        ember_kernel,
        out_shape=(struct(12, 4, NZ), struct(CX * CY, NZ)),
        in_specs=[VMEM] * 3,
        out_specs=(VMEM, VMEM),
        scratch_shapes=[
            pltpu.VMEM((6, 8, CAP), jnp.float32),
            pltpu.VMEM((4, CX * CY, 2 * NZ), jnp.bfloat16),
            pltpu.VMEM((CX * CY, CAP), jnp.float32),
            pltpu.VMEM((6, 8, CAP), jnp.float32),
        ],
        compiler_params=PARAMS,
        cost_estimate=pl.CostEstimate(flops=5_000_000_000, bytes_accessed=0, transcendentals=0),
        name="embers",
    )(fields, e1, e2)
    advanced, _, _ = pl.pallas_call(
        far_kernel,
        out_shape=(struct(4, CX, CY, NZ), tile, tile),
        in_specs=[SMEM] + [VMEM] * 7,
        out_specs=(VMEM, VMEM, VMEM),
        input_output_aliases={6: 1, 7: 2},
        compiler_params=PARAMS,
        name="far",
    )(flags, ub, db, ua, da, deposit.reshape(CX, CY, NZ), a, b)
    return (advanced, landed.reshape(4, 1, 1, 6, CAP))


def solution(mesh):
    placed = (
        P(None, "down", "cross", None),
        P(None, "down", "cross", None, None),
        P("down", "cross", None),
    )
    return jax.shard_map(
        local,
        mesh=mesh,
        in_specs=placed,
        out_specs=(P(None, "down", "cross", None), P(None, "down", "cross", None, None)),
        check_vma=False,
    )
```

```python
import jax
import jax.numpy as jnp
from jax import lax
from jax.experimental import pallas as pl
from jax.experimental.pallas import tpu as pltpu
from jax.sharding import PartitionSpec as P

STEPS = 6
HORIZONTAL_MIX = 0.1
VERTICAL_MIX = 0.1
ADVECTION = 0.25
DRAG_RATE = 0.6
BURN_RATE = 0.5
HEAT_YIELD = 4.0

CX, CY, NZ = 8, 64, 128
CAP = 256
H = STEPS
NEAR = 3
FAR = H - NEAR
PAD = 16
WIDE = CY + 2 * PAD
TALL = CX + 2 * H
TOP = H - NEAR
CORNER = {1: 0, 3: 5, 2: 8, 4: 12, 5: 14}
B_CORN = 32 * NEAR
A_BLOCKS = B_CORN + 16
C_RECS = 32
C_BLOCKS = 36

HBM = pl.BlockSpec(memory_space=pltpu.HBM)
VMEM = pl.BlockSpec(memory_space=pltpu.VMEM)
SMEM = pl.BlockSpec(memory_space=pltpu.SMEM)
ANY = pl.BlockSpec(memory_space=pl.ANY)


def corner_entry(k, dist, side):
    return B_CORN + (2 * k + CORNER[dist] // 8) * 2 + side


def edge_kernel(
    counts_ref, embers_ref, fields_hbm, cp_ref, cm_ref, own_ref, fields_ref, counts, embers, sems
):
    copies = [
        pltpu.make_async_copy(counts_ref, counts, sems.at[0]),
        pltpu.make_async_copy(embers_ref, embers, sems.at[1]),
        pltpu.make_async_copy(fields_hbm, fields_ref, sems.at[2]),
    ]
    for copy in copies:
        copy.start()
    for copy in copies[:2]:
        copy.wait()
    lane = lax.broadcasted_iota(jnp.int32, (1, NZ), 1)
    for slot in range(6):
        base, target = ((C_RECS, cm_ref), (0, own_ref), (C_RECS, cp_ref))[slot % 3]
        for half in range(2):
            live = (lane + NZ * half < counts[0, 0, slot]).astype(jnp.float32)
            for comp in range(7):
                row = comp * 12 + slot * 2 + half
                put = comp * 4 + slot // 3 * 2 + half
                target[base + put // 8, put % 8 : put % 8 + 1, :] = (
                    embers[row // 4, row % 4 : row % 4 + 1, :] * live
                )
    for base, target in ((C_RECS, cm_ref), (0, own_ref), (C_RECS, cp_ref)):
        target[base + 3, 4:8, :] = jnp.zeros((4, NZ), jnp.float32)
    copies[2].wait()
    for k in range(4):
        for row in range(CX):
            cp_ref[8 * k + row] = fields_ref[k, row, CY - 8 :, :]
            cm_ref[8 * k + row] = fields_ref[k, row, 0:8, :]


def records_kernel(cp_ref, cm_ref, own_ref, e1_ref, e2_ref):
    for which, target in ((0, e1_ref), (1, e2_ref)):
        for j, base, ref in ((0, C_RECS, cm_ref), (1, 0, own_ref), (2, C_RECS, cp_ref)):
            for comp in range(7):
                for half in range(2):
                    row = comp * 4 + which * 2 + half
                    put = comp * 6 + j * 2 + half
                    target[put // 8, put % 8 : put % 8 + 1, :] = ref[
                        base + row // 8, row % 8 : row % 8 + 1, :
                    ]
        target[5, 2:8, :] = jnp.zeros((6, NZ), jnp.float32)


def pack_kernel(fields_ref, cp_ref, cm_ref, ua_ref, da_ref):
    for k in range(4):
        for i in range(NEAR):
            for j in range(8):
                at = (k * NEAR + i) * 8 + j
                ua_ref[at] = fields_ref[k, CX - NEAR + i, 8 * j : 8 * j + 8, :]
                da_ref[at] = fields_ref[k, i, 8 * j : 8 * j + 8, :]
        for ref, up in ((ua_ref, True), (da_ref, False)):
            for dist, first in CORNER.items():
                cols = H - dist
                at = first % 8
                row = CX - dist if up else dist - 1
                ref[corner_entry(k, dist, 0), at : at + cols, :] = cp_ref[
                    8 * k + row, 8 - cols : 8, :
                ]
                ref[corner_entry(k, dist, 1), at : at + cols, :] = cm_ref[8 * k + row, 0:cols, :]
            for side in range(2):
                ref[corner_entry(k, 5, side), 7:8, :] = jnp.zeros((1, NZ), jnp.float32)


def far_pack_kernel(fields_ref, ub_ref, db_ref):
    for k in range(4):
        for i in range(FAR):
            ub_ref[k, i] = fields_ref[k, CX - H + i]
            db_ref[k, i] = fields_ref[k, NEAR + i]


def split(x):
    high = x.astype(jnp.bfloat16)
    low = (x - high.astype(jnp.float32)).astype(jnp.bfloat16)
    return high, low


def dot32(a, b):
    return lax.dot_general(a, b, (((1,), (0,)), ((), ())), preferred_element_type=jnp.float32)


def dot32t(a, b):
    return lax.dot_general(a, b, (((1,), (1,)), ((), ())), preferred_element_type=jnp.float32)


def tent(position, count):
    centre = lax.broadcasted_iota(jnp.int32, (count, CAP), 0).astype(jnp.float32) + 0.5
    return jnp.maximum(0.0, 1.0 - jnp.abs(position - centre))


def ember_kernel(
    fields_ref, e1_ref, e2_ref, landed_ref, deposit_ref, rec, parts, weight, fate
):
    cells = CX * CY
    for k in range(4):
        high, low = split(fields_ref[k].reshape(cells, NZ))
        parts[k, :, 0:NZ] = high
        parts[k, :, NZ:] = low
    deposit_ref[...] = jnp.zeros_like(deposit_ref)
    for slot in range(6):
        ref = e1_ref if slot < 3 else e2_ref
        for comp in range(7):
            for half in range(2):
                row = comp * 6 + slot % 3 * 2 + half
                rec[slot, comp : comp + 1, NZ * half : NZ * half + NZ] = ref[
                    row // 8, row % 8 : row % 8 + 1, :
                ]

    @pl.loop(0, 6)
    def _(slot):
        field = [rec[slot, i : i + 1, :] for i in range(7)]
        down = tent(field[0] * CX, CX)
        cross = tent(field[1] * CY, CY)
        level = tent(field[2] * NZ, NZ)
        for x in range(CX):
            weight[CY * x : CY * x + CY, :] = down[x : x + 1, :] * cross
        level_high, level_low = split(level)
        both = jnp.concatenate([level_high, level_high], axis=0)
        sampled = []
        for k in range(4):
            column = dot32(parts[k], both) + dot32(parts[k, :, 0:NZ], level_low)
            sampled.append(jnp.sum(column * weight[...], axis=0, keepdims=True))
        mass = field[5]
        heat = field[6] + sampled[2] - sampled[3]
        burned = mass * BURN_RATE * jax.nn.sigmoid(heat)
        living = (mass > 0.0).astype(jnp.float32)
        fate[slot, 0:1, :] = (field[3] + DRAG_RATE * (sampled[0] - field[3])) * living
        fate[slot, 1:2, :] = (field[4] + DRAG_RATE * (sampled[1] - field[4])) * living
        fate[slot, 2:3, :] = (field[6] + DRAG_RATE * (sampled[2] - field[6])) * living
        fate[slot, 3:4, :] = (mass - burned) * living
        heat_high, heat_low = split(level * (HEAT_YIELD * burned))
        weight_high, weight_low = split(weight[...])
        extra = (
            dot32t(weight_high, heat_high)
            + dot32t(weight_high, heat_low)
            + dot32t(weight_low, heat_high)
        )
        deposit_ref[...] += extra

    for slot in range(6):
        for i in range(4):
            for half in range(2):
                row = i * 12 + slot * 2 + half
                landed_ref[row // 4, row % 4 : row % 4 + 1, :] = fate[
                    slot, i : i + 1, NZ * half : NZ * half + NZ
                ]


def edges():
    lane = lax.broadcasted_iota(jnp.int32, (8, NZ), 1)
    return lane == 0, lane == NZ - 1


def cell_block(src, row, col, scale, ends):
    first_level, last_level = ends
    half_step = ADVECTION * 0.5 * scale
    mix = HORIZONTAL_MIX * scale
    u = src[0, row, col : col + 8, :] * half_step
    v = src[1, row, col : col + 8, :] * half_step
    east, west, north, south = (mix - u, mix + u, mix - v, mix + v)
    keep = (1.0 - 4.0 * HORIZONTAL_MIX - 2.0 * VERTICAL_MIX) * scale
    column = VERTICAL_MIX * scale
    out = []
    for k in range(4):
        f = src[k, row, col : col + 8, :]
        above = jnp.where(last_level, f, pltpu.roll(f, NZ - 1, 1))
        below = jnp.where(first_level, f, pltpu.roll(f, 1, 1))
        out.append(
            (keep * f + column * (above + below))
            + (east * src[k, row + 1, col : col + 8, :] + west * src[k, row - 1, col : col + 8, :])
            + (
                north * src[k, row, col + 1 : col + 9, :]
                + south * src[k, row, col - 1 : col + 7, :]
            )
        )
    return out


def wide_row(flags_ref, src, dst, row, ends):
    inside = jnp.where(row < H, flags_ref[0], jnp.where(row >= H + CX, flags_ref[1], 1))
    inside = inside.astype(jnp.float32)
    left, right = (flags_ref[2].astype(jnp.float32), flags_ref[3].astype(jnp.float32))
    for block in range(10):
        col = 8 + 8 * block
        scale = inside * left if block == 0 else inside * right if block == 9 else inside
        for k, value in enumerate(cell_block(src, row, col, scale, ends)):
            dst[k, row, col : col + 8, :] = value


def fill_sides(a, rows, ua_ref, da_ref):
    zero = jnp.zeros((PAD, NZ), jnp.float32)
    for k in range(4):
        for row in rows:
            a[k, row, 0:PAD, :] = zero
            a[k, row, PAD + CY :, :] = zero
            ref, dist = (ua_ref, H - row) if row < H else (da_ref, row - (H + CX - 1))
            if dist in CORNER:
                cols, at = H - dist, CORNER[dist] % 8
                a[k, row, PAD - cols : PAD, :] = ref[corner_entry(k, dist, 0), at : at + cols, :]
                a[k, row, PAD + CY : PAD + CY + cols, :] = ref[
                    corner_entry(k, dist, 1), at : at + cols, :
                ]


def near_kernel(flags_ref, fields_ref, ua_ref, da_ref, cp_ref, cm_ref, a, b, sem):
    copy = pltpu.make_async_copy(fields_ref, a.at[:, H : H + CX, PAD : PAD + CY, :], sem)
    copy.start()
    edge = jnp.zeros((8, NZ), jnp.float32)
    for k in range(4):
        for row in range(CX):
            a[k, H + row, 0:8, :] = edge
            a[k, H + row, 8:16, :] = cp_ref[8 * k + row]
            a[k, H + row, PAD + CY : PAD + CY + 8, :] = cm_ref[8 * k + row]
            a[k, H + row, PAD + CY + 8 :, :] = edge
        for i in range(NEAR):
            for j in range(8):
                at = (k * NEAR + i) * 8 + j
                a[k, TOP + i, PAD + 8 * j : PAD + 8 * j + 8, :] = ua_ref[at]
                a[k, H + CX + i, PAD + 8 * j : PAD + 8 * j + 8, :] = da_ref[at]
        for row in range(TALL):
            b[k, row, 0:8, :] = edge
            b[k, row, PAD + CY + 8 :, :] = edge
    fill_sides(a, (*range(TOP, H), *range(H + CX, H + CX + NEAR)), ua_ref, da_ref)
    copy.wait()
    ends = edges()
    for step in range(1, STEPS + 1):
        src, dst = (a, b) if step % 2 == 1 else (b, a)
        if TOP + step < TALL - TOP - step:

            @pl.loop(TOP + step, TALL - TOP - step)
            def _(row):
                wide_row(flags_ref, src, dst, row, ends)


def far_kernel(
    flags_ref, ub_ref, db_ref, ua_ref, da_ref, deposit_ref, a_in, b_in, out_ref, a, b
):
    fill_sides(a, (*range(FAR), *range(TALL - FAR, TALL)), ua_ref, da_ref)
    for k in range(4):
        for i in range(FAR):
            a[k, i, PAD : PAD + CY, :] = ub_ref[k, i]
            a[k, TALL - FAR + i, PAD : PAD + CY, :] = db_ref[k, i]
    ends = edges()
    for step in range(1, STEPS):
        src, dst = (a, b) if step % 2 == 1 else (b, a)

        @pl.loop(0, FAR)
        def _(i):
            wide_row(flags_ref, src, dst, i + step, ends)
            wide_row(flags_ref, src, dst, TALL - 1 - step - i, ends)

    src, dst = (a, b) if STEPS % 2 == 1 else (b, a)

    def last_row(row, values):
        for block in range(8):
            for k, value in enumerate(values(row, PAD + 8 * block)):
                if k == 2:
                    value = value + deposit_ref[row, 8 * block : 8 * block + 8, :]
                out_ref[k, row, 8 * block : 8 * block + 8, :] = value

    def computed(row, col):
        return cell_block(src, row + H, col, 1.0, ends)

    def kept(row, col):
        return [dst[k, row + H, col : col + 8, :] for k in range(4)]

    done = range(H - NEAR, NEAR + CX - H)
    if len(done):

        @pl.loop(0, done.start)
        def _(row):
            last_row(row, computed)
            last_row(CX - 1 - row, computed)

        for row in done:
            last_row(row, kept)
    else:

        @pl.loop(0, CX)
        def _(row):
            last_row(row, computed)


def struct(*shape):
    return jax.ShapeDtypeStruct(shape, jnp.float32)


def moved(x, axis, by):
    size = lax.axis_size(axis)
    pairs = [(i, i + by) for i in range(size) if 0 <= i + by < size]
    return lax.ppermute(x, axis, pairs)


PARAMS = pltpu.CompilerParams(vmem_limit_bytes=32 * 1024 * 1024)


def local(fields, embers, counts):
    down, cross = (lax.axis_index("down"), lax.axis_index("cross"))
    flags = jnp.stack(
        [
            down > 0,
            down < lax.axis_size("down") - 1,
            cross > 0,
            cross < lax.axis_size("cross") - 1,
        ]
    ).astype(jnp.int32)
    cp, cm, own, fields = pl.pallas_call(
        edge_kernel,
        out_shape=(
            struct(C_BLOCKS, 8, NZ),
            struct(C_BLOCKS, 8, NZ),
            struct(4, 8, NZ),
            struct(4, CX, CY, NZ),
        ),
        in_specs=[HBM, HBM, HBM],
        out_specs=(VMEM,) * 4,
        scratch_shapes=[
            pltpu.SMEM((1, 1, 6), jnp.int32),
            pltpu.VMEM((21, 4, NZ), jnp.float32),
            pltpu.SemaphoreType.DMA((3,)),
        ],
        compiler_params=PARAMS,
        name="edges",
    )(counts, embers.reshape(21, 4, NZ), fields)
    cp = moved(cp, "cross", 1)
    cm = moved(cm, "cross", -1)
    e1, e2 = pl.pallas_call(
        records_kernel,
        out_shape=(struct(6, 8, NZ), struct(6, 8, NZ)),
        in_specs=[VMEM] * 3,
        out_specs=(VMEM, VMEM),
        compiler_params=PARAMS,
        name="records",
    )(cp, cm, own)
    fields, e1, e2 = lax.optimization_barrier((fields, e1, e2))
    ub, db = pl.pallas_call(
        far_pack_kernel,
        out_shape=(struct(4, FAR, CY, NZ), struct(4, FAR, CY, NZ)),
        in_specs=[VMEM],
        out_specs=(VMEM, VMEM),
        compiler_params=PARAMS,
        name="far_pack",
    )(fields)
    e1 = moved(e1, "down", 1)
    e2 = moved(e2, "down", 2)
    ua, da = pl.pallas_call(
        pack_kernel,
        out_shape=(struct(A_BLOCKS, 8, NZ), struct(A_BLOCKS, 8, NZ)),
        in_specs=[VMEM] * 3,
        out_specs=(VMEM, VMEM),
        compiler_params=PARAMS,
        name="pack",
    )(fields, cp, cm)
    ua = moved(ua, "down", 1)
    da = moved(da, "down", -1)
    ub = moved(ub, "down", 1)
    db = moved(db, "down", -1)
    tile = struct(4, TALL, WIDE, NZ)
    a, b = pl.pallas_call(
        near_kernel,
        out_shape=(tile, tile),
        in_specs=[SMEM, ANY, VMEM, VMEM, VMEM, VMEM],
        out_specs=(VMEM, VMEM),
        scratch_shapes=[pltpu.SemaphoreType.DMA],
        compiler_params=PARAMS,
        cost_estimate=pl.CostEstimate(flops=1_000_000_000, bytes_accessed=0, transcendentals=0),
        name="near",
    )(flags, fields, ua, da, cp, cm)
    a, b, e1, e2 = lax.optimization_barrier((a, b, e1, e2))
    landed, deposit = pl.pallas_call(
        ember_kernel,
        out_shape=(struct(12, 4, NZ), struct(CX * CY, NZ)),
        in_specs=[VMEM] * 3,
        out_specs=(VMEM, VMEM),
        scratch_shapes=[
            pltpu.VMEM((6, 8, CAP), jnp.float32),
            pltpu.VMEM((4, CX * CY, 2 * NZ), jnp.bfloat16),
            pltpu.VMEM((CX * CY, CAP), jnp.float32),
            pltpu.VMEM((6, 8, CAP), jnp.float32),
        ],
        compiler_params=PARAMS,
        cost_estimate=pl.CostEstimate(flops=5_000_000_000, bytes_accessed=0, transcendentals=0),
        name="embers",
    )(fields, e1, e2)
    advanced, _, _ = pl.pallas_call(
        far_kernel,
        out_shape=(struct(4, CX, CY, NZ), tile, tile),
        in_specs=[SMEM] + [VMEM] * 7,
        out_specs=(VMEM, VMEM, VMEM),
        input_output_aliases={6: 1, 7: 2},
        compiler_params=PARAMS,
        name="far",
    )(flags, ub, db, ua, da, deposit.reshape(CX, CY, NZ), a, b)
    return (advanced, landed.reshape(4, 1, 1, 6, CAP))


def solution(mesh):
    placed = (
        P(None, "down", "cross", None),
        P(None, "down", "cross", None, None),
        P("down", "cross", None),
    )
    return jax.shard_map(
        local,
        mesh=mesh,
        in_specs=placed,
        out_specs=(P(None, "down", "cross", None), P(None, "down", "cross", None, None)),
        check_vma=False,
    )
```

```python
import jax
import jax.numpy as jnp
from jax import lax
from jax.experimental import pallas as pl
from jax.experimental.pallas import tpu as pltpu
from jax.sharding import PartitionSpec as P

STEPS = 6
HORIZONTAL_MIX = 0.1
VERTICAL_MIX = 0.1
ADVECTION = 0.25
DRAG_RATE = 0.6
BURN_RATE = 0.5
HEAT_YIELD = 4.0

CX, CY, NZ = 8, 64, 128
CAP = 256
H = STEPS
NEAR = 2
FAR = H - NEAR
PAD = 16
WIDE = CY + 2 * PAD
TALL = CX + 2 * H
TOP = H - NEAR
CORNER = {1: 0, 3: 5, 2: 8, 4: 12, 5: 14}
B_CORN = 32 * NEAR
A_BLOCKS = B_CORN + 16
C_RECS = 32
C_BLOCKS = 36

HBM = pl.BlockSpec(memory_space=pltpu.HBM)
VMEM = pl.BlockSpec(memory_space=pltpu.VMEM)
SMEM = pl.BlockSpec(memory_space=pltpu.SMEM)
ANY = pl.BlockSpec(memory_space=pl.ANY)


def corner_entry(k, dist, side):
    return B_CORN + (2 * k + CORNER[dist] // 8) * 2 + side


def edge_kernel(
    counts_ref, embers_ref, fields_hbm, cp_ref, cm_ref, own_ref, fields_ref, counts, embers, sems
):
    copies = [
        pltpu.make_async_copy(counts_ref, counts, sems.at[0]),
        pltpu.make_async_copy(embers_ref, embers, sems.at[1]),
        pltpu.make_async_copy(fields_hbm, fields_ref, sems.at[2]),
    ]
    for copy in copies:
        copy.start()
    for copy in copies[:2]:
        copy.wait()
    lane = lax.broadcasted_iota(jnp.int32, (1, NZ), 1)
    for slot in range(6):
        base, target = ((C_RECS, cm_ref), (0, own_ref), (C_RECS, cp_ref))[slot % 3]
        for half in range(2):
            live = (lane + NZ * half < counts[0, 0, slot]).astype(jnp.float32)
            for comp in range(7):
                row = comp * 12 + slot * 2 + half
                put = comp * 4 + slot // 3 * 2 + half
                target[base + put // 8, put % 8 : put % 8 + 1, :] = (
                    embers[row // 4, row % 4 : row % 4 + 1, :] * live
                )
    for base, target in ((C_RECS, cm_ref), (0, own_ref), (C_RECS, cp_ref)):
        target[base + 3, 4:8, :] = jnp.zeros((4, NZ), jnp.float32)
    copies[2].wait()
    for k in range(4):
        for row in range(CX):
            cp_ref[8 * k + row] = fields_ref[k, row, CY - 8 :, :]
            cm_ref[8 * k + row] = fields_ref[k, row, 0:8, :]


def records_kernel(cp_ref, cm_ref, own_ref, e1_ref, e2_ref):
    for which, target in ((0, e1_ref), (1, e2_ref)):
        for j, base, ref in ((0, C_RECS, cm_ref), (1, 0, own_ref), (2, C_RECS, cp_ref)):
            for comp in range(7):
                for half in range(2):
                    row = comp * 4 + which * 2 + half
                    put = comp * 6 + j * 2 + half
                    target[put // 8, put % 8 : put % 8 + 1, :] = ref[
                        base + row // 8, row % 8 : row % 8 + 1, :
                    ]
        target[5, 2:8, :] = jnp.zeros((6, NZ), jnp.float32)


def pack_kernel(fields_ref, cp_ref, cm_ref, ua_ref, da_ref):
    for k in range(4):
        for i in range(NEAR):
            for j in range(8):
                at = (k * NEAR + i) * 8 + j
                ua_ref[at] = fields_ref[k, CX - NEAR + i, 8 * j : 8 * j + 8, :]
                da_ref[at] = fields_ref[k, i, 8 * j : 8 * j + 8, :]
        for ref, up in ((ua_ref, True), (da_ref, False)):
            for dist, first in CORNER.items():
                cols = H - dist
                at = first % 8
                row = CX - dist if up else dist - 1
                ref[corner_entry(k, dist, 0), at : at + cols, :] = cp_ref[
                    8 * k + row, 8 - cols : 8, :
                ]
                ref[corner_entry(k, dist, 1), at : at + cols, :] = cm_ref[8 * k + row, 0:cols, :]
            for side in range(2):
                ref[corner_entry(k, 5, side), 7:8, :] = jnp.zeros((1, NZ), jnp.float32)


def far_pack_kernel(fields_ref, ub_ref, db_ref):
    for k in range(4):
        for i in range(FAR):
            ub_ref[k, i] = fields_ref[k, CX - H + i]
            db_ref[k, i] = fields_ref[k, NEAR + i]


def split(x):
    high = x.astype(jnp.bfloat16)
    low = (x - high.astype(jnp.float32)).astype(jnp.bfloat16)
    return high, low


def dot32(a, b):
    return lax.dot_general(a, b, (((1,), (0,)), ((), ())), preferred_element_type=jnp.float32)


def dot32t(a, b):
    return lax.dot_general(a, b, (((1,), (1,)), ((), ())), preferred_element_type=jnp.float32)


def tent(position, count):
    centre = lax.broadcasted_iota(jnp.int32, (count, CAP), 0).astype(jnp.float32) + 0.5
    return jnp.maximum(0.0, 1.0 - jnp.abs(position - centre))


def ember_kernel(
    fields_ref, e1_ref, e2_ref, landed_ref, deposit_ref, rec, parts, weight, fate
):
    cells = CX * CY
    for k in range(4):
        high, low = split(fields_ref[k].reshape(cells, NZ))
        parts[k, :, 0:NZ] = high
        parts[k, :, NZ:] = low
    deposit_ref[...] = jnp.zeros_like(deposit_ref)
    for slot in range(6):
        ref = e1_ref if slot < 3 else e2_ref
        for comp in range(7):
            for half in range(2):
                row = comp * 6 + slot % 3 * 2 + half
                rec[slot, comp : comp + 1, NZ * half : NZ * half + NZ] = ref[
                    row // 8, row % 8 : row % 8 + 1, :
                ]

    @pl.loop(0, 6)
    def _(slot):
        field = [rec[slot, i : i + 1, :] for i in range(7)]
        down = tent(field[0] * CX, CX)
        cross = tent(field[1] * CY, CY)
        level = tent(field[2] * NZ, NZ)
        for x in range(CX):
            weight[CY * x : CY * x + CY, :] = down[x : x + 1, :] * cross
        level_high, level_low = split(level)
        both = jnp.concatenate([level_high, level_high], axis=0)
        sampled = []
        for k in range(4):
            column = dot32(parts[k], both) + dot32(parts[k, :, 0:NZ], level_low)
            sampled.append(jnp.sum(column * weight[...], axis=0, keepdims=True))
        mass = field[5]
        heat = field[6] + sampled[2] - sampled[3]
        burned = mass * BURN_RATE * jax.nn.sigmoid(heat)
        living = (mass > 0.0).astype(jnp.float32)
        fate[slot, 0:1, :] = (field[3] + DRAG_RATE * (sampled[0] - field[3])) * living
        fate[slot, 1:2, :] = (field[4] + DRAG_RATE * (sampled[1] - field[4])) * living
        fate[slot, 2:3, :] = (field[6] + DRAG_RATE * (sampled[2] - field[6])) * living
        fate[slot, 3:4, :] = (mass - burned) * living
        heat_high, heat_low = split(level * (HEAT_YIELD * burned))
        weight_high, weight_low = split(weight[...])
        extra = (
            dot32t(weight_high, heat_high)
            + dot32t(weight_high, heat_low)
            + dot32t(weight_low, heat_high)
        )
        deposit_ref[...] += extra

    for slot in range(6):
        for i in range(4):
            for half in range(2):
                row = i * 12 + slot * 2 + half
                landed_ref[row // 4, row % 4 : row % 4 + 1, :] = fate[
                    slot, i : i + 1, NZ * half : NZ * half + NZ
                ]


def edges():
    lane = lax.broadcasted_iota(jnp.int32, (8, NZ), 1)
    return lane == 0, lane == NZ - 1


def cell_block(src, row, col, scale, ends):
    first_level, last_level = ends
    half_step = ADVECTION * 0.5 * scale
    mix = HORIZONTAL_MIX * scale
    u = src[0, row, col : col + 8, :] * half_step
    v = src[1, row, col : col + 8, :] * half_step
    east, west, north, south = (mix - u, mix + u, mix - v, mix + v)
    keep = (1.0 - 4.0 * HORIZONTAL_MIX - 2.0 * VERTICAL_MIX) * scale
    column = VERTICAL_MIX * scale
    out = []
    for k in range(4):
        f = src[k, row, col : col + 8, :]
        above = jnp.where(last_level, f, pltpu.roll(f, NZ - 1, 1))
        below = jnp.where(first_level, f, pltpu.roll(f, 1, 1))
        out.append(
            (keep * f + column * (above + below))
            + (east * src[k, row + 1, col : col + 8, :] + west * src[k, row - 1, col : col + 8, :])
            + (
                north * src[k, row, col + 1 : col + 9, :]
                + south * src[k, row, col - 1 : col + 7, :]
            )
        )
    return out


def wide_row(flags_ref, src, dst, row, ends):
    inside = jnp.where(row < H, flags_ref[0], jnp.where(row >= H + CX, flags_ref[1], 1))
    inside = inside.astype(jnp.float32)
    left, right = (flags_ref[2].astype(jnp.float32), flags_ref[3].astype(jnp.float32))
    for block in range(10):
        col = 8 + 8 * block
        scale = inside * left if block == 0 else inside * right if block == 9 else inside
        for k, value in enumerate(cell_block(src, row, col, scale, ends)):
            dst[k, row, col : col + 8, :] = value


def fill_sides(a, rows, ua_ref, da_ref):
    zero = jnp.zeros((PAD, NZ), jnp.float32)
    for k in range(4):
        for row in rows:
            a[k, row, 0:PAD, :] = zero
            a[k, row, PAD + CY :, :] = zero
            ref, dist = (ua_ref, H - row) if row < H else (da_ref, row - (H + CX - 1))
            if dist in CORNER:
                cols, at = H - dist, CORNER[dist] % 8
                a[k, row, PAD - cols : PAD, :] = ref[corner_entry(k, dist, 0), at : at + cols, :]
                a[k, row, PAD + CY : PAD + CY + cols, :] = ref[
                    corner_entry(k, dist, 1), at : at + cols, :
                ]


def near_kernel(flags_ref, fields_ref, ua_ref, da_ref, cp_ref, cm_ref, a, b, sem):
    copy = pltpu.make_async_copy(fields_ref, a.at[:, H : H + CX, PAD : PAD + CY, :], sem)
    copy.start()
    edge = jnp.zeros((8, NZ), jnp.float32)
    for k in range(4):
        for row in range(CX):
            a[k, H + row, 0:8, :] = edge
            a[k, H + row, 8:16, :] = cp_ref[8 * k + row]
            a[k, H + row, PAD + CY : PAD + CY + 8, :] = cm_ref[8 * k + row]
            a[k, H + row, PAD + CY + 8 :, :] = edge
        for i in range(NEAR):
            for j in range(8):
                at = (k * NEAR + i) * 8 + j
                a[k, TOP + i, PAD + 8 * j : PAD + 8 * j + 8, :] = ua_ref[at]
                a[k, H + CX + i, PAD + 8 * j : PAD + 8 * j + 8, :] = da_ref[at]
        for row in range(TALL):
            b[k, row, 0:8, :] = edge
            b[k, row, PAD + CY + 8 :, :] = edge
    fill_sides(a, (*range(TOP, H), *range(H + CX, H + CX + NEAR)), ua_ref, da_ref)
    copy.wait()
    ends = edges()
    for step in range(1, STEPS + 1):
        src, dst = (a, b) if step % 2 == 1 else (b, a)
        if TOP + step < TALL - TOP - step:

            @pl.loop(TOP + step, TALL - TOP - step)
            def _(row):
                wide_row(flags_ref, src, dst, row, ends)


def far_kernel(
    flags_ref, ub_ref, db_ref, ua_ref, da_ref, deposit_ref, a_in, b_in, out_ref, a, b
):
    fill_sides(a, (*range(FAR), *range(TALL - FAR, TALL)), ua_ref, da_ref)
    for k in range(4):
        for i in range(FAR):
            a[k, i, PAD : PAD + CY, :] = ub_ref[k, i]
            a[k, TALL - FAR + i, PAD : PAD + CY, :] = db_ref[k, i]
    ends = edges()
    for step in range(1, STEPS):
        src, dst = (a, b) if step % 2 == 1 else (b, a)

        @pl.loop(0, FAR)
        def _(i):
            wide_row(flags_ref, src, dst, i + step, ends)
            wide_row(flags_ref, src, dst, TALL - 1 - step - i, ends)

    src, dst = (a, b) if STEPS % 2 == 1 else (b, a)

    def last_row(row, values):
        for block in range(8):
            for k, value in enumerate(values(row, PAD + 8 * block)):
                if k == 2:
                    value = value + deposit_ref[row, 8 * block : 8 * block + 8, :]
                out_ref[k, row, 8 * block : 8 * block + 8, :] = value

    def computed(row, col):
        return cell_block(src, row + H, col, 1.0, ends)

    def kept(row, col):
        return [dst[k, row + H, col : col + 8, :] for k in range(4)]

    done = range(H - NEAR, NEAR + CX - H)
    if len(done):

        @pl.loop(0, done.start)
        def _(row):
            last_row(row, computed)
            last_row(CX - 1 - row, computed)

        for row in done:
            last_row(row, kept)
    else:

        @pl.loop(0, CX)
        def _(row):
            last_row(row, computed)


def struct(*shape):
    return jax.ShapeDtypeStruct(shape, jnp.float32)


def moved(x, axis, by):
    size = lax.axis_size(axis)
    pairs = [(i, i + by) for i in range(size) if 0 <= i + by < size]
    return lax.ppermute(x, axis, pairs)


PARAMS = pltpu.CompilerParams(vmem_limit_bytes=32 * 1024 * 1024)


def local(fields, embers, counts):
    down, cross = (lax.axis_index("down"), lax.axis_index("cross"))
    flags = jnp.stack(
        [
            down > 0,
            down < lax.axis_size("down") - 1,
            cross > 0,
            cross < lax.axis_size("cross") - 1,
        ]
    ).astype(jnp.int32)
    cp, cm, own, fields = pl.pallas_call(
        edge_kernel,
        out_shape=(
            struct(C_BLOCKS, 8, NZ),
            struct(C_BLOCKS, 8, NZ),
            struct(4, 8, NZ),
            struct(4, CX, CY, NZ),
        ),
        in_specs=[HBM, HBM, HBM],
        out_specs=(VMEM,) * 4,
        scratch_shapes=[
            pltpu.SMEM((1, 1, 6), jnp.int32),
            pltpu.VMEM((21, 4, NZ), jnp.float32),
            pltpu.SemaphoreType.DMA((3,)),
        ],
        compiler_params=PARAMS,
        name="edges",
    )(counts, embers.reshape(21, 4, NZ), fields)
    cp = moved(cp, "cross", 1)
    cm = moved(cm, "cross", -1)
    e1, e2 = pl.pallas_call(
        records_kernel,
        out_shape=(struct(6, 8, NZ), struct(6, 8, NZ)),
        in_specs=[VMEM] * 3,
        out_specs=(VMEM, VMEM),
        compiler_params=PARAMS,
        name="records",
    )(cp, cm, own)
    fields, e1, e2 = lax.optimization_barrier((fields, e1, e2))
    ub, db = pl.pallas_call(
        far_pack_kernel,
        out_shape=(struct(4, FAR, CY, NZ), struct(4, FAR, CY, NZ)),
        in_specs=[VMEM],
        out_specs=(VMEM, VMEM),
        compiler_params=PARAMS,
        name="far_pack",
    )(fields)
    e1 = moved(e1, "down", 1)
    e2 = moved(e2, "down", 2)
    ua, da = pl.pallas_call(
        pack_kernel,
        out_shape=(struct(A_BLOCKS, 8, NZ), struct(A_BLOCKS, 8, NZ)),
        in_specs=[VMEM] * 3,
        out_specs=(VMEM, VMEM),
        compiler_params=PARAMS,
        name="pack",
    )(fields, cp, cm)
    ua = moved(ua, "down", 1)
    da = moved(da, "down", -1)
    ub = moved(ub, "down", 1)
    db = moved(db, "down", -1)
    tile = struct(4, TALL, WIDE, NZ)
    a, b = pl.pallas_call(
        near_kernel,
        out_shape=(tile, tile),
        in_specs=[SMEM, ANY, VMEM, VMEM, VMEM, VMEM],
        out_specs=(VMEM, VMEM),
        scratch_shapes=[pltpu.SemaphoreType.DMA],
        compiler_params=PARAMS,
        cost_estimate=pl.CostEstimate(flops=1_000_000_000, bytes_accessed=0, transcendentals=0),
        name="near",
    )(flags, fields, ua, da, cp, cm)
    a, b, e1, e2 = lax.optimization_barrier((a, b, e1, e2))
    landed, deposit = pl.pallas_call(
        ember_kernel,
        out_shape=(struct(12, 4, NZ), struct(CX * CY, NZ)),
        in_specs=[VMEM] * 3,
        out_specs=(VMEM, VMEM),
        scratch_shapes=[
            pltpu.VMEM((6, 8, CAP), jnp.float32),
            pltpu.VMEM((4, CX * CY, 2 * NZ), jnp.bfloat16),
            pltpu.VMEM((CX * CY, CAP), jnp.float32),
            pltpu.VMEM((6, 8, CAP), jnp.float32),
        ],
        compiler_params=PARAMS,
        cost_estimate=pl.CostEstimate(flops=5_000_000_000, bytes_accessed=0, transcendentals=0),
        name="embers",
    )(fields, e1, e2)
    advanced, _, _ = pl.pallas_call(
        far_kernel,
        out_shape=(struct(4, CX, CY, NZ), tile, tile),
        in_specs=[SMEM] + [VMEM] * 7,
        out_specs=(VMEM, VMEM, VMEM),
        input_output_aliases={6: 1, 7: 2},
        compiler_params=PARAMS,
        name="far",
    )(flags, ub, db, ua, da, deposit.reshape(CX, CY, NZ), a, b)
    return (advanced, landed.reshape(4, 1, 1, 6, CAP))


def solution(mesh):
    placed = (
        P(None, "down", "cross", None),
        P(None, "down", "cross", None, None),
        P("down", "cross", None),
    )
    return jax.shard_map(
        local,
        mesh=mesh,
        in_specs=placed,
        out_specs=(P(None, "down", "cross", None), P(None, "down", "cross", None, None)),
        check_vma=False,
    )
```

```python
import jax
import jax.numpy as jnp
from jax import lax
from jax.experimental import pallas as pl
from jax.experimental.pallas import tpu as pltpu
from jax.sharding import PartitionSpec as P

STEPS = 6
HORIZONTAL_MIX = 0.1
VERTICAL_MIX = 0.1
ADVECTION = 0.25
DRAG_RATE = 0.6
BURN_RATE = 0.5
HEAT_YIELD = 4.0

CX, CY, NZ = 8, 64, 128
CAP = 256
H = STEPS
NEAR = 1
FAR = H - NEAR
PAD = 16
WIDE = CY + 2 * PAD
TALL = CX + 2 * H
TOP = H - NEAR
CORNER = {1: 0, 3: 5, 2: 8, 4: 12, 5: 14}
B_CORN = 32 * NEAR
A_BLOCKS = B_CORN + 16
C_RECS = 32
C_BLOCKS = 36

HBM = pl.BlockSpec(memory_space=pltpu.HBM)
VMEM = pl.BlockSpec(memory_space=pltpu.VMEM)
SMEM = pl.BlockSpec(memory_space=pltpu.SMEM)
ANY = pl.BlockSpec(memory_space=pl.ANY)


def corner_entry(k, dist, side):
    return B_CORN + (2 * k + CORNER[dist] // 8) * 2 + side


def edge_kernel(
    counts_ref, embers_ref, fields_hbm, cp_ref, cm_ref, own_ref, fields_ref, counts, embers, sems
):
    copies = [
        pltpu.make_async_copy(counts_ref, counts, sems.at[0]),
        pltpu.make_async_copy(embers_ref, embers, sems.at[1]),
        pltpu.make_async_copy(fields_hbm, fields_ref, sems.at[2]),
    ]
    for copy in copies:
        copy.start()
    for copy in copies[:2]:
        copy.wait()
    lane = lax.broadcasted_iota(jnp.int32, (1, NZ), 1)
    for slot in range(6):
        base, target = ((C_RECS, cm_ref), (0, own_ref), (C_RECS, cp_ref))[slot % 3]
        for half in range(2):
            live = (lane + NZ * half < counts[0, 0, slot]).astype(jnp.float32)
            for comp in range(7):
                row = comp * 12 + slot * 2 + half
                put = comp * 4 + slot // 3 * 2 + half
                target[base + put // 8, put % 8 : put % 8 + 1, :] = (
                    embers[row // 4, row % 4 : row % 4 + 1, :] * live
                )
    for base, target in ((C_RECS, cm_ref), (0, own_ref), (C_RECS, cp_ref)):
        target[base + 3, 4:8, :] = jnp.zeros((4, NZ), jnp.float32)
    copies[2].wait()
    for k in range(4):
        for row in range(CX):
            cp_ref[8 * k + row] = fields_ref[k, row, CY - 8 :, :]
            cm_ref[8 * k + row] = fields_ref[k, row, 0:8, :]


def records_kernel(cp_ref, cm_ref, own_ref, e1_ref, e2_ref):
    for which, target in ((0, e1_ref), (1, e2_ref)):
        for j, base, ref in ((0, C_RECS, cm_ref), (1, 0, own_ref), (2, C_RECS, cp_ref)):
            for comp in range(7):
                for half in range(2):
                    row = comp * 4 + which * 2 + half
                    put = comp * 6 + j * 2 + half
                    target[put // 8, put % 8 : put % 8 + 1, :] = ref[
                        base + row // 8, row % 8 : row % 8 + 1, :
                    ]
        target[5, 2:8, :] = jnp.zeros((6, NZ), jnp.float32)


def pack_kernel(fields_ref, cp_ref, cm_ref, ua_ref, da_ref):
    for k in range(4):
        for i in range(NEAR):
            for j in range(8):
                at = (k * NEAR + i) * 8 + j
                ua_ref[at] = fields_ref[k, CX - NEAR + i, 8 * j : 8 * j + 8, :]
                da_ref[at] = fields_ref[k, i, 8 * j : 8 * j + 8, :]
        for ref, up in ((ua_ref, True), (da_ref, False)):
            for dist, first in CORNER.items():
                cols = H - dist
                at = first % 8
                row = CX - dist if up else dist - 1
                ref[corner_entry(k, dist, 0), at : at + cols, :] = cp_ref[
                    8 * k + row, 8 - cols : 8, :
                ]
                ref[corner_entry(k, dist, 1), at : at + cols, :] = cm_ref[8 * k + row, 0:cols, :]
            for side in range(2):
                ref[corner_entry(k, 5, side), 7:8, :] = jnp.zeros((1, NZ), jnp.float32)


def far_pack_kernel(fields_ref, ub_ref, db_ref):
    for k in range(4):
        for i in range(FAR):
            ub_ref[k, i] = fields_ref[k, CX - H + i]
            db_ref[k, i] = fields_ref[k, NEAR + i]


def split(x):
    high = x.astype(jnp.bfloat16)
    low = (x - high.astype(jnp.float32)).astype(jnp.bfloat16)
    return high, low


def dot32(a, b):
    return lax.dot_general(a, b, (((1,), (0,)), ((), ())), preferred_element_type=jnp.float32)


def dot32t(a, b):
    return lax.dot_general(a, b, (((1,), (1,)), ((), ())), preferred_element_type=jnp.float32)


def tent(position, count):
    centre = lax.broadcasted_iota(jnp.int32, (count, CAP), 0).astype(jnp.float32) + 0.5
    return jnp.maximum(0.0, 1.0 - jnp.abs(position - centre))


def ember_kernel(
    fields_ref, e1_ref, e2_ref, landed_ref, deposit_ref, rec, parts, weight, fate
):
    cells = CX * CY
    for k in range(4):
        high, low = split(fields_ref[k].reshape(cells, NZ))
        parts[k, :, 0:NZ] = high
        parts[k, :, NZ:] = low
    deposit_ref[...] = jnp.zeros_like(deposit_ref)
    for slot in range(6):
        ref = e1_ref if slot < 3 else e2_ref
        for comp in range(7):
            for half in range(2):
                row = comp * 6 + slot % 3 * 2 + half
                rec[slot, comp : comp + 1, NZ * half : NZ * half + NZ] = ref[
                    row // 8, row % 8 : row % 8 + 1, :
                ]

    @pl.loop(0, 6)
    def _(slot):
        field = [rec[slot, i : i + 1, :] for i in range(7)]
        down = tent(field[0] * CX, CX)
        cross = tent(field[1] * CY, CY)
        level = tent(field[2] * NZ, NZ)
        for x in range(CX):
            weight[CY * x : CY * x + CY, :] = down[x : x + 1, :] * cross
        level_high, level_low = split(level)
        both = jnp.concatenate([level_high, level_high], axis=0)
        sampled = []
        for k in range(4):
            column = dot32(parts[k], both) + dot32(parts[k, :, 0:NZ], level_low)
            sampled.append(jnp.sum(column * weight[...], axis=0, keepdims=True))
        mass = field[5]
        heat = field[6] + sampled[2] - sampled[3]
        burned = mass * BURN_RATE * jax.nn.sigmoid(heat)
        living = (mass > 0.0).astype(jnp.float32)
        fate[slot, 0:1, :] = (field[3] + DRAG_RATE * (sampled[0] - field[3])) * living
        fate[slot, 1:2, :] = (field[4] + DRAG_RATE * (sampled[1] - field[4])) * living
        fate[slot, 2:3, :] = (field[6] + DRAG_RATE * (sampled[2] - field[6])) * living
        fate[slot, 3:4, :] = (mass - burned) * living
        heat_high, heat_low = split(level * (HEAT_YIELD * burned))
        weight_high, weight_low = split(weight[...])
        extra = (
            dot32t(weight_high, heat_high)
            + dot32t(weight_high, heat_low)
            + dot32t(weight_low, heat_high)
        )
        deposit_ref[...] += extra

    for slot in range(6):
        for i in range(4):
            for half in range(2):
                row = i * 12 + slot * 2 + half
                landed_ref[row // 4, row % 4 : row % 4 + 1, :] = fate[
                    slot, i : i + 1, NZ * half : NZ * half + NZ
                ]


def edges():
    lane = lax.broadcasted_iota(jnp.int32, (8, NZ), 1)
    return lane == 0, lane == NZ - 1


def cell_block(src, row, col, scale, ends):
    first_level, last_level = ends
    half_step = ADVECTION * 0.5 * scale
    mix = HORIZONTAL_MIX * scale
    u = src[0, row, col : col + 8, :] * half_step
    v = src[1, row, col : col + 8, :] * half_step
    east, west, north, south = (mix - u, mix + u, mix - v, mix + v)
    keep = (1.0 - 4.0 * HORIZONTAL_MIX - 2.0 * VERTICAL_MIX) * scale
    column = VERTICAL_MIX * scale
    out = []
    for k in range(4):
        f = src[k, row, col : col + 8, :]
        above = jnp.where(last_level, f, pltpu.roll(f, NZ - 1, 1))
        below = jnp.where(first_level, f, pltpu.roll(f, 1, 1))
        out.append(
            (keep * f + column * (above + below))
            + (east * src[k, row + 1, col : col + 8, :] + west * src[k, row - 1, col : col + 8, :])
            + (
                north * src[k, row, col + 1 : col + 9, :]
                + south * src[k, row, col - 1 : col + 7, :]
            )
        )
    return out


def wide_row(flags_ref, src, dst, row, ends):
    inside = jnp.where(row < H, flags_ref[0], jnp.where(row >= H + CX, flags_ref[1], 1))
    inside = inside.astype(jnp.float32)
    left, right = (flags_ref[2].astype(jnp.float32), flags_ref[3].astype(jnp.float32))
    for block in range(10):
        col = 8 + 8 * block
        scale = inside * left if block == 0 else inside * right if block == 9 else inside
        for k, value in enumerate(cell_block(src, row, col, scale, ends)):
            dst[k, row, col : col + 8, :] = value


def fill_sides(a, rows, ua_ref, da_ref):
    zero = jnp.zeros((PAD, NZ), jnp.float32)
    for k in range(4):
        for row in rows:
            a[k, row, 0:PAD, :] = zero
            a[k, row, PAD + CY :, :] = zero
            ref, dist = (ua_ref, H - row) if row < H else (da_ref, row - (H + CX - 1))
            if dist in CORNER:
                cols, at = H - dist, CORNER[dist] % 8
                a[k, row, PAD - cols : PAD, :] = ref[corner_entry(k, dist, 0), at : at + cols, :]
                a[k, row, PAD + CY : PAD + CY + cols, :] = ref[
                    corner_entry(k, dist, 1), at : at + cols, :
                ]


def near_kernel(flags_ref, fields_ref, ua_ref, da_ref, cp_ref, cm_ref, a, b, sem):
    copy = pltpu.make_async_copy(fields_ref, a.at[:, H : H + CX, PAD : PAD + CY, :], sem)
    copy.start()
    edge = jnp.zeros((8, NZ), jnp.float32)
    for k in range(4):
        for row in range(CX):
            a[k, H + row, 0:8, :] = edge
            a[k, H + row, 8:16, :] = cp_ref[8 * k + row]
            a[k, H + row, PAD + CY : PAD + CY + 8, :] = cm_ref[8 * k + row]
            a[k, H + row, PAD + CY + 8 :, :] = edge
        for i in range(NEAR):
            for j in range(8):
                at = (k * NEAR + i) * 8 + j
                a[k, TOP + i, PAD + 8 * j : PAD + 8 * j + 8, :] = ua_ref[at]
                a[k, H + CX + i, PAD + 8 * j : PAD + 8 * j + 8, :] = da_ref[at]
        for row in range(TALL):
            b[k, row, 0:8, :] = edge
            b[k, row, PAD + CY + 8 :, :] = edge
    fill_sides(a, (*range(TOP, H), *range(H + CX, H + CX + NEAR)), ua_ref, da_ref)
    copy.wait()
    ends = edges()
    for step in range(1, STEPS + 1):
        src, dst = (a, b) if step % 2 == 1 else (b, a)
        if TOP + step < TALL - TOP - step:

            @pl.loop(TOP + step, TALL - TOP - step)
            def _(row):
                wide_row(flags_ref, src, dst, row, ends)


def far_kernel(
    flags_ref, ub_ref, db_ref, ua_ref, da_ref, deposit_ref, a_in, b_in, out_ref, a, b
):
    fill_sides(a, (*range(FAR), *range(TALL - FAR, TALL)), ua_ref, da_ref)
    for k in range(4):
        for i in range(FAR):
            a[k, i, PAD : PAD + CY, :] = ub_ref[k, i]
            a[k, TALL - FAR + i, PAD : PAD + CY, :] = db_ref[k, i]
    ends = edges()
    for step in range(1, STEPS):
        src, dst = (a, b) if step % 2 == 1 else (b, a)

        @pl.loop(0, FAR)
        def _(i):
            wide_row(flags_ref, src, dst, i + step, ends)
            wide_row(flags_ref, src, dst, TALL - 1 - step - i, ends)

    src, dst = (a, b) if STEPS % 2 == 1 else (b, a)

    def last_row(row, values):
        for block in range(8):
            for k, value in enumerate(values(row, PAD + 8 * block)):
                if k == 2:
                    value = value + deposit_ref[row, 8 * block : 8 * block + 8, :]
                out_ref[k, row, 8 * block : 8 * block + 8, :] = value

    def computed(row, col):
        return cell_block(src, row + H, col, 1.0, ends)

    def kept(row, col):
        return [dst[k, row + H, col : col + 8, :] for k in range(4)]

    done = range(H - NEAR, NEAR + CX - H)
    if len(done):

        @pl.loop(0, done.start)
        def _(row):
            last_row(row, computed)
            last_row(CX - 1 - row, computed)

        for row in done:
            last_row(row, kept)
    else:

        @pl.loop(0, CX)
        def _(row):
            last_row(row, computed)


def struct(*shape):
    return jax.ShapeDtypeStruct(shape, jnp.float32)


def moved(x, axis, by):
    size = lax.axis_size(axis)
    pairs = [(i, i + by) for i in range(size) if 0 <= i + by < size]
    return lax.ppermute(x, axis, pairs)


PARAMS = pltpu.CompilerParams(vmem_limit_bytes=32 * 1024 * 1024)


def local(fields, embers, counts):
    down, cross = (lax.axis_index("down"), lax.axis_index("cross"))
    flags = jnp.stack(
        [
            down > 0,
            down < lax.axis_size("down") - 1,
            cross > 0,
            cross < lax.axis_size("cross") - 1,
        ]
    ).astype(jnp.int32)
    cp, cm, own, fields = pl.pallas_call(
        edge_kernel,
        out_shape=(
            struct(C_BLOCKS, 8, NZ),
            struct(C_BLOCKS, 8, NZ),
            struct(4, 8, NZ),
            struct(4, CX, CY, NZ),
        ),
        in_specs=[HBM, HBM, HBM],
        out_specs=(VMEM,) * 4,
        scratch_shapes=[
            pltpu.SMEM((1, 1, 6), jnp.int32),
            pltpu.VMEM((21, 4, NZ), jnp.float32),
            pltpu.SemaphoreType.DMA((3,)),
        ],
        compiler_params=PARAMS,
        name="edges",
    )(counts, embers.reshape(21, 4, NZ), fields)
    cp = moved(cp, "cross", 1)
    cm = moved(cm, "cross", -1)
    e1, e2 = pl.pallas_call(
        records_kernel,
        out_shape=(struct(6, 8, NZ), struct(6, 8, NZ)),
        in_specs=[VMEM] * 3,
        out_specs=(VMEM, VMEM),
        compiler_params=PARAMS,
        name="records",
    )(cp, cm, own)
    fields, e1, e2 = lax.optimization_barrier((fields, e1, e2))
    ub, db = pl.pallas_call(
        far_pack_kernel,
        out_shape=(struct(4, FAR, CY, NZ), struct(4, FAR, CY, NZ)),
        in_specs=[VMEM],
        out_specs=(VMEM, VMEM),
        compiler_params=PARAMS,
        name="far_pack",
    )(fields)
    e1 = moved(e1, "down", 1)
    e2 = moved(e2, "down", 2)
    ua, da = pl.pallas_call(
        pack_kernel,
        out_shape=(struct(A_BLOCKS, 8, NZ), struct(A_BLOCKS, 8, NZ)),
        in_specs=[VMEM] * 3,
        out_specs=(VMEM, VMEM),
        compiler_params=PARAMS,
        name="pack",
    )(fields, cp, cm)
    ua = moved(ua, "down", 1)
    da = moved(da, "down", -1)
    ub = moved(ub, "down", 1)
    db = moved(db, "down", -1)
    tile = struct(4, TALL, WIDE, NZ)
    a, b = pl.pallas_call(
        near_kernel,
        out_shape=(tile, tile),
        in_specs=[SMEM, ANY, VMEM, VMEM, VMEM, VMEM],
        out_specs=(VMEM, VMEM),
        scratch_shapes=[pltpu.SemaphoreType.DMA],
        compiler_params=PARAMS,
        cost_estimate=pl.CostEstimate(flops=1_000_000_000, bytes_accessed=0, transcendentals=0),
        name="near",
    )(flags, fields, ua, da, cp, cm)
    a, b, e1, e2 = lax.optimization_barrier((a, b, e1, e2))
    landed, deposit = pl.pallas_call(
        ember_kernel,
        out_shape=(struct(12, 4, NZ), struct(CX * CY, NZ)),
        in_specs=[VMEM] * 3,
        out_specs=(VMEM, VMEM),
        scratch_shapes=[
            pltpu.VMEM((6, 8, CAP), jnp.float32),
            pltpu.VMEM((4, CX * CY, 2 * NZ), jnp.bfloat16),
            pltpu.VMEM((CX * CY, CAP), jnp.float32),
            pltpu.VMEM((6, 8, CAP), jnp.float32),
        ],
        compiler_params=PARAMS,
        cost_estimate=pl.CostEstimate(flops=8_000_000_000, bytes_accessed=0, transcendentals=0),
        name="embers",
    )(fields, e1, e2)
    advanced, _, _ = pl.pallas_call(
        far_kernel,
        out_shape=(struct(4, CX, CY, NZ), tile, tile),
        in_specs=[SMEM] + [VMEM] * 7,
        out_specs=(VMEM, VMEM, VMEM),
        input_output_aliases={6: 1, 7: 2},
        compiler_params=PARAMS,
        name="far",
    )(flags, ub, db, ua, da, deposit.reshape(CX, CY, NZ), a, b)
    return (advanced, landed.reshape(4, 1, 1, 6, CAP))


def solution(mesh):
    placed = (
        P(None, "down", "cross", None),
        P(None, "down", "cross", None, None),
        P("down", "cross", None),
    )
    return jax.shard_map(
        local,
        mesh=mesh,
        in_specs=placed,
        out_specs=(P(None, "down", "cross", None), P(None, "down", "cross", None, None)),
        check_vma=False,
    )
```
